512 devices in a mesh: segment: 64 (over z_lo, y, core), head: 8 (over x, z_hi).
Axes of the slice: x: 4, y: 8, z: 8 (z_hi: 2, z_lo: 4; z = z_hi * 4 + z_lo), core: 2. Of those that a mesh axis runs over, the one named last changes fastest.
Arguments:
- segment_rows: bfloat16 [2, 8192, 2048], P(None, 'segment', 'head'), may hold values from -6 to 6
- row_cotangent: bfloat16 [2, 8192, 2048], P(None, 'segment', 'head'), may hold values from -6 to 6
- memory_gain: float32 [2048], P('head'), may hold values from 0.5 to 1.5
- cross_gain: float32 [2048], P('head'), may hold values from 0.5 to 1.5
- w_query: bfloat16 [2048, 2048], P('segment', 'head'), may hold values from -0.125 to 0.125
- w_key: bfloat16 [2048, 2048], P('segment', 'head'), may hold values from -0.125 to 0.125
- w_value: bfloat16 [2048, 2048], P('segment', 'head'), may hold values from -0.125 to 0.125
- w_out: bfloat16 [2048, 2048], P('head', 'segment'), may hold values from -0.125 to 0.125
Outputs:
- segment_result: bfloat16 [2, 8192, 2048], P(None, 'segment', 'head')
The draws below stay inside these ranges and needn't reach their ends.
All inputs are finite; a program needn't handle non-finite values.
Results may differ from the reference program's by a relative error of at most 0.0065.
Values may be sent and summed in bfloat16 or wider, within the bound.
A program may use at most 64 MiB of HBM per device.

```python
import jax
import jax.numpy as jnp
from jax import lax

D = 2048
HEADS = 32
HS = 64
MB = 2
ROWS = 128
PAIRS = 32
TOTAL = 8192


def level_of(stream_key, dims, pieces, low, top_value):
    level, own = 1.0, jax.random.fold_in(stream_key, 6)
    for dim, blocks in pieces:
        draws = jnp.exp(jax.random.uniform(jax.random.fold_in(own, dim), (blocks,), jnp.float32, low / len(pieces), top_value / len(pieces)))
        level = level * jnp.repeat(draws, dims[dim] // blocks).reshape([-1 if axis == dim else 1 for axis in range(len(dims))])
    return level


def gaussian(key, shape, scale, reach, shards=(), kind=jnp.bfloat16):
    drawn = jax.random.normal(key, shape, jnp.float32) * scale
    if len(shards) > 0:
        drawn = level_of(key, shape, shards, -0.22, 0.18) * drawn
    return jnp.clip(drawn, min=-reach, max=reach).astype(kind)


def setup_inputs(seed: int = 0) -> dict:
    splits = jax.random.split(jax.random.key(seed), 9)
    segment_rows = gaussian(splits[0], (MB, TOTAL, D), 1.0, 6.0, ((1, 64), (2, 8)))
    row_cotangent = gaussian(splits[1], (MB, TOTAL, D), 1.0, 6.0, ((1, 64), (2, 8)))
    memory_gain = jnp.clip(1.0 + 0.1 * jax.random.normal(splits[2], (D,), jnp.float32), 0.5, 1.5)
    cross_gain = jnp.clip(1.0 + 0.1 * jax.random.normal(splits[3], (D,), jnp.float32), 0.5, 1.5)
    w_query = gaussian(splits[4], (D, HEADS * HS), D ** -0.5, 0.125, ((0, 64), (1, 8)))
    w_key = gaussian(splits[5], (D, HEADS * HS), D ** -0.5, 0.125, ((0, 64), (1, 8)))
    w_value = gaussian(splits[6], (D, HEADS * HS), D ** -0.5, 0.125, ((0, 64), (1, 8)))
    w_out = gaussian(splits[7], (HEADS * HS, D), (HEADS * HS) ** -0.5, 0.125, ((0, 8), (1, 64)))
    return {"segment_rows": segment_rows, "row_cotangent": row_cotangent, "memory_gain": memory_gain, "cross_gain": cross_gain, "w_query": w_query, "w_key": w_key, "w_value": w_value, "w_out": w_out}


EPS = 1e-06

def norm_rows(block, gain_vec):
    block_f = block.astype(jnp.float32)
    inv_norm = lax.rsqrt(lax.optimization_barrier(jnp.mean(block_f * block_f, axis=-1, keepdims=True)) + EPS)
    return ((block_f * inv_norm * gain_vec).astype(jnp.bfloat16), inv_norm)

def reference(segment_rows, row_cotangent, memory_gain, cross_gain, w_query, w_key, w_value, w_out):
    half_rows = PAIRS * ROWS
    enc_rows = segment_rows[:, :half_rows].reshape(MB, PAIRS, ROWS, D)
    dec_rows = segment_rows[:, half_rows:].reshape(MB, PAIRS, ROWS, D)
    enc_cot = row_cotangent[:, :half_rows].reshape(MB, PAIRS, ROWS, D)
    dec_cot = row_cotangent[:, half_rows:].reshape(MB, PAIRS, ROWS, D)
    memory, inv_enc = norm_rows(enc_rows, memory_gain)
    normed, inv_dec = norm_rows(dec_rows, cross_gain)
    flat_mem = memory.reshape(-1, D)
    head_shape = (MB, PAIRS, ROWS, HEADS, HS)
    query_rows = jnp.dot(normed.reshape(-1, D), w_query, preferred_element_type=jnp.float32).astype(jnp.bfloat16).reshape(head_shape)
    key_rows = jnp.dot(flat_mem, w_key, preferred_element_type=jnp.float32).astype(jnp.bfloat16).reshape(head_shape)
    value_rows = jnp.dot(flat_mem, w_value, preferred_element_type=jnp.float32).astype(jnp.bfloat16).reshape(head_shape)
    factor = HS ** (-0.5)
    scores = jnp.einsum('bpqhd,bpkhd->bphqk', query_rows.astype(jnp.float32), key_rows.astype(jnp.float32)) * factor
    weights_f = jax.nn.softmax(scores, axis=-1)
    weights_low = weights_f.astype(jnp.bfloat16)
    attended = jnp.einsum('bphqk,bpkhd->bpqhd', weights_low.astype(jnp.float32), value_rows.astype(jnp.float32)).astype(jnp.bfloat16)
    mixed = jnp.dot(attended.reshape(-1, HEADS * HS), w_out, preferred_element_type=jnp.float32).reshape(MB, PAIRS, ROWS, D)
    decoded = (dec_rows.astype(jnp.float32) + mixed).astype(jnp.bfloat16)
    d_att = jnp.dot(dec_cot.reshape(-1, D), w_out.T, preferred_element_type=jnp.float32).astype(jnp.bfloat16).reshape(head_shape)
    d_weights = jnp.einsum('bpqhd,bpkhd->bphqk', d_att.astype(jnp.float32), value_rows.astype(jnp.float32))
    d_scores = weights_f * (d_weights - lax.optimization_barrier(jnp.sum(weights_f * d_weights, axis=-1, keepdims=True)))
    d_low = (d_scores * factor).astype(jnp.bfloat16)
    d_key = jnp.einsum('bphqk,bpqhd->bpkhd', d_low.astype(jnp.float32), query_rows.astype(jnp.float32)).astype(jnp.bfloat16)
    d_value = jnp.einsum('bphqk,bpqhd->bpkhd', weights_low.astype(jnp.float32), d_att.astype(jnp.float32)).astype(jnp.bfloat16)
    d_memory = jnp.dot(d_key.reshape(-1, HEADS * HS), w_key.T, preferred_element_type=jnp.float32)
    d_memory = d_memory + jnp.dot(d_value.reshape(-1, HEADS * HS), w_value.T, preferred_element_type=jnp.float32)
    d_memory = d_memory.reshape(MB, PAIRS, ROWS, D) + enc_cot.astype(jnp.float32)
    enc_f = enc_rows.astype(jnp.float32)
    weighted = d_memory * memory_gain
    inner = lax.optimization_barrier(jnp.mean(enc_f * weighted, axis=-1, keepdims=True))
    d_enc = (inv_enc * weighted - enc_f * inv_enc ** 3 * inner).astype(jnp.bfloat16)
    return jnp.concatenate([d_enc.reshape(MB, half_rows, D), decoded.reshape(MB, half_rows, D)], axis=1)
```

```python
import functools

import jax
import jax.numpy as jnp
from jax import lax
from jax.experimental import pallas as pl
from jax.experimental.pallas import tpu as pltpu
from jax.sharding import PartitionSpec as P

D = 2048
HS = 64
EPS = 1e-06
NX = 4
NY = 8
NT = (((1,), (1,)), ((), ()))
TN = (((0,), (0,)), ((), ()))
F32 = jnp.float32
BF16 = jnp.bfloat16

W_Z = 0
W_RIGHT = 3
W_LEFT = 19
W_MATE = 35
A_ROWS = 43
A_COT = 46
A_AUX = 49
A_RIGHT = 52
A_LEFT = 55
X_AUX = 58
S_OUT = 61
S_STAT = 73
F_SUM = 76
F_STAT = 79
COPIES = 82


def dot(a, b, dims=(((1,), (0,)), ((), ()))):
    return lax.dot_general(a, b, dims, preferred_element_type=F32)


def kernel(
    rows, cot, mgain, cgain, wq, wk, wv, wo, out,
    w, act, aux, hold, stage, near, far, stat_out, stat_in, last, last_in, last_stat, stat_last,
    ssem, rsem,
):
    seg = lax.axis_index("segment")
    head = lax.axis_index("head")
    c = seg % 2
    y = (seg // 2) % NY
    zl = seg // (2 * NY)
    p = zl % 2
    side = zl // 2
    x = head // 2
    zh = head % 2
    oh = 1 - zh
    other = 1 - side

    def at(x_=x, y_=y, zl_=zl, zh_=zh, c_=c):
        return ((zl_ * NY + y_) * 2 + c_, x_ * 2 + zh_)

    xr, xl, xx = (x + 1) % NX, (x + NX - 1) % NX, (x + 2) % NX
    right, left, across = at(x_=xr), at(x_=xl), at(x_=xx)
    up, down = at(y_=(y + 1) % NY), at(y_=(y + NY - 1) % NY)
    mate = at(c_=1 - c)
    zl_of = (zl, (1 - p) + 2 * side, p + 2 * other, (1 - p) + 2 * other)
    w_to = [None] + [at(zl_=v) for v in zl_of[1:]]
    r1, r2, r3 = at(zl_=zl_of[2]), at(zh_=oh), at(zl_=zl_of[2], zh_=oh)

    def copy(src, dst, number, to):
        return pltpu.make_async_remote_copy(
            src_ref=src, dst_ref=dst, send_sem=ssem.at[number], recv_sem=rsem.at[number],
            device_id=to, device_id_type=pl.DeviceIdType.MESH,
        )

    pending = []

    def send(src, dst, number, to):
        one = copy(src, dst, number, to)
        one.start()
        pending.append(one)

    def arrived(dst, number):
        copy(dst, dst, number, mate).wait_recv()

    eye = lax.broadcasted_iota(jnp.int32, (128, 128), 0) == lax.broadcasted_iota(
        jnp.int32, (128, 128), 1
    )

    def as_row(col):
        return jnp.sum(jnp.where(eye, col, 0.0), axis=0, keepdims=True)

    def as_col(row):
        return jnp.sum(jnp.where(eye, row, 0.0), axis=1, keepdims=True)

    barrier = pltpu.get_barrier_semaphore()
    partners = (right, left, across, up, down, mate, r1, r2, r3, w_to[1], w_to[3])
    for partner in partners:
        pl.semaphore_signal(
            barrier, inc=1, device_id=partner, device_id_type=pl.DeviceIdType.MESH
        )
    w[zl, y, c, :, 0:256] = wq[...]
    w[zl, y, c, :, 256:512] = wk[...]
    w[zl, y, c, :, 512:768] = wv[...]
    w[zl, y, c, :, 768:1024] = jnp.transpose(wo[...].astype(F32)).astype(BF16)
    act[side, x, zh] = rows[side]

    @pl.when(side == 1)
    def _():
        act[2, x, zh] = cot[1]

    @pl.when(side == 0)
    def _():
        aux[x, zh, 0:1, :] = mgain[...]
        aux[x, zh, 1:2, :] = cgain[...]
        for m in range(2):
            inner = rows[m].astype(F32) * cot[m].astype(F32) * mgain[...]
            aux[x, zh, 2:3, 128 * m : 128 * m + 128] = as_row(
                jnp.sum(inner, axis=1, keepdims=True)
            )
        aux[x, zh, 3:8, :] = jnp.zeros((5, 256), F32)

    pl.semaphore_wait(barrier, len(partners))

    own = w.at[zl, y, c]
    for d in (2, 1, 3):
        send(own, own, W_Z + d - 1, w_to[d])
    send(own, own, W_RIGHT, up)
    send(own, own, W_LEFT, down)

    mine = act.at[side, x, zh]
    send(rows.at[other], mine, A_ROWS, r1)
    send(rows.at[other], mine, A_ROWS + 2, r3)
    send(rows.at[side], mine, A_ROWS + 1, r2)
    my_cot = act.at[2, x, zh]
    my_aux = aux.at[x, zh]
    cots = [
        copy(cot.at[0], my_cot, A_COT, r1),
        copy(cot.at[0], my_cot, A_COT + 2, r3),
        copy(cot.at[1], my_cot, A_COT + 1, r2),
    ]
    auxes = [copy(my_aux, my_aux, A_AUX + i, to) for i, to in enumerate((r1, r2, r3))]

    @pl.when(side == 1)
    def _():
        for one in cots:
            one.start()

    @pl.when(side == 0)
    def _():
        for one in auxes:
            one.start()

    def up_down(t, d):
        if t < 4 or d < 2:
            block = w.at[zl_of[d], (y + NY - t + 1) % NY, c]
            send(block, block, W_RIGHT + 4 * (t - 1) + d, up)
        if t < 4 or d >= 2:
            block = w.at[zl_of[d], (y + t - 1) % NY, c]
            send(block, block, W_LEFT + 4 * (t - 1) + d, down)

    def from_ring(t, d):
        if t < 4 or d < 2:
            arrived(w.at[zl_of[d], (y + NY - t) % NY, c], W_RIGHT + 4 * (t - 1) + d)
        if t < 4 or d >= 2:
            arrived(w.at[zl_of[d], (y + t) % NY, c], W_LEFT + 4 * (t - 1) + d)

    def share(number):
        block = w.at[:, (y + number) % NY, c]
        send(block, block, W_MATE + number, mate)

    for d in (1, 2, 3):
        arrived(w.at[zl_of[d], y, c], W_Z + d - 1)
        up_down(1, d)
    share(0)

    def group(x_, g):
        return act.at[:, x_, oh if g else zh]

    arrived(act.at[other, x, zh], A_ROWS)

    @pl.when(side == 0)
    def _():
        arrived(act.at[2, x, zh], A_COT)

    send(group(x, 0), group(x, 0), A_RIGHT, right)
    send(group(x, 0), group(x, 0), A_LEFT, left)
    arrived(act.at[side, x, oh], A_ROWS + 1)
    arrived(act.at[other, x, oh], A_ROWS + 2)

    @pl.when(side == 0)
    def _():
        arrived(act.at[2, x, oh], A_COT + 2)
        arrived(aux.at[x, oh], A_AUX + 1)

    @pl.when(side == 1)
    def _():
        arrived(act.at[2, x, oh], A_COT + 1)
        arrived(aux.at[x, zh], A_AUX)
        arrived(aux.at[x, oh], A_AUX + 2)

    send(group(x, 1), group(x, 1), A_RIGHT + 1, right)
    send(group(x, 1), group(x, 1), A_LEFT + 1, left)
    for i, to in enumerate((right, left, across)):
        send(aux.at[x], aux.at[x], X_AUX + i, to)

    for d in range(4):
        from_ring(1, d)
        up_down(2, d)
    share(1)
    share(7)

    arrived(group(xl, 0), A_RIGHT)
    send(group(xl, 0), group(xl, 0), A_RIGHT + 2, right)
    arrived(group(xr, 0), A_LEFT)
    arrived(group(xl, 1), A_RIGHT + 1)
    arrived(group(xr, 1), A_LEFT + 1)
    send(group(xr, 1), group(xr, 1), A_LEFT + 2, left)

    for d in range(4):
        from_ring(2, d)
        up_down(3, d)
    share(2)
    share(6)
    for d in range(4):
        from_ring(3, d)
        up_down(4, d)
    share(3)
    share(5)
    for d in range(4):
        from_ring(4, d)
    share(4)

    arrived(group(xx, 0), A_RIGHT + 2)
    arrived(group(xx, 1), A_LEFT + 2)
    for i, x_ in enumerate((xl, xr, xx)):
        arrived(aux.at[x_], X_AUX + i)
    for number in range(NY):
        arrived(w.at[:, (y + number) % NY, 1 - c], W_MATE + number)

    blocks = [(i // 2, i % 2) for i in range(8)]

    def inverse(kind):
        total = jnp.zeros((128, 256), F32)
        for i, j in blocks:
            v = act[kind, i, j].astype(F32)
            total = total + v * v
        return lax.rsqrt(jnp.sum(total, axis=1, keepdims=True) / D + EPS)

    inv_e = inverse(0)
    inv_x = inverse(1)
    kv = jnp.zeros((128, 512), F32)
    q = jnp.zeros((128, 256), F32)
    da = jnp.zeros((128, 256), F32)
    c_inner = jnp.zeros((1, 256), F32)
    for i, j in blocks:
        memory = (act[0, i, j].astype(F32) * inv_e * aux[i, j, 0:1, :]).astype(BF16)
        normed = (act[1, i, j].astype(F32) * inv_x * aux[i, j, 1:2, :]).astype(BF16)
        part = w.at[i, 4 * j : 4 * j + 4]
        kv = kv + dot(memory, part[:, :, :, 256:768].reshape(256, 512))
        q = q + dot(normed, part[:, :, :, 0:256].reshape(256, 256))
        da = da + dot(act[2, i, j], part[:, :, :, 768:1024].reshape(256, 256))
        c_inner = c_inner + aux[i, j, 2:3, :]
    kv = kv.astype(BF16).astype(F32)
    q = q.astype(BF16).astype(F32)
    da = da.astype(BF16).astype(F32)
    c_inner = jnp.where(side == 0, c_inner[:, 0:128], c_inner[:, 128:256])

    low = lax.broadcasted_iota(jnp.int32, (128, 128), 1) < HS
    factor = HS ** (-0.5)

    def two(v):
        return jnp.concatenate(
            [jnp.where(low, v, 0.0).astype(BF16), jnp.where(low, 0.0, v).astype(BF16)], axis=0
        )

    attended, saved = [], []
    for pair in range(2):
        lanes = slice(128 * pair, 128 * pair + 128)
        q2 = two(q[:, lanes])
        key = kv[:, lanes].astype(BF16)
        value = kv[:, 256 + 128 * pair : 384 + 128 * pair]
        scores = dot(q2, key, NT) * factor
        e = jnp.exp(scores - jnp.max(scores, axis=1, keepdims=True))
        probs = e / jnp.sum(e, axis=1, keepdims=True)
        probs_low = probs.astype(BF16)
        v2 = two(value)
        attended.append(dot(probs_low[:128], v2[:128]) + dot(probs_low[128:], v2[128:]))
        saved.append((q2, value.astype(BF16), probs, probs_low, two(da[:, lanes])))
    attended = jnp.concatenate(attended, axis=1).astype(BF16)

    def weight_rows(x_, j, lanes):
        return w[x_, 4 * j : 4 * j + 4, :, :, lanes].reshape(256, lanes.stop - lanes.start)

    def hand_out(kind, chunk):
        base = S_OUT + 6 * kind
        stage[kind, 0] = chunk(xx, 0).astype(BF16)
        send(stage.at[kind, 0], far.at[kind, 0], base, right)
        stage[kind, 1] = chunk(xx, 1).astype(BF16)
        send(stage.at[kind, 1], far.at[kind, 1], base + 1, left)
        stage[kind, 2] = chunk(xr, 1).astype(BF16)
        send(stage.at[kind, 2], near.at[kind, 0], base + 2, right)
        stage[kind, 3] = chunk(xl, 0).astype(BF16)
        send(stage.at[kind, 3], near.at[kind, 1], base + 3, left)
        hold[kind, 0] = chunk(xr, 0)
        hold[kind, 1] = chunk(xl, 1)
        hold[kind, 2] = chunk(x, 0)
        hold[kind, 3] = chunk(x, 1)

    def pass_on(kind):
        base = S_OUT + 6 * kind
        for i, to in enumerate((right, left)):
            arrived(far.at[kind, i], base + i)
            stage[kind, 4 + i] = (hold[kind, i] + far[kind, i].astype(F32)).astype(BF16)
            send(stage.at[kind, 4 + i], near.at[kind, 2 + i], base + 4 + i, to)

    def finish(kind):
        base = S_OUT + 6 * kind
        for i in range(4):
            arrived(near.at[kind, i], base + 2 + i)
        hold[kind, 2] = hold[kind, 2] + near[kind, 2].astype(F32) + near[kind, 1].astype(F32)
        hold[kind, 3] = hold[kind, 3] + near[kind, 0].astype(F32) + near[kind, 3].astype(F32)
        for i in range(2):
            last[kind, i] = hold[kind, 2 + i].astype(BF16)

    hand_out(1, lambda x_, j: dot(attended, weight_rows(x_, j, slice(768, 1024)), NT))

    d_keys, d_values = [], []
    for q2, value, probs, probs_low, da2 in saved:
        d_probs = dot(da2, value, NT)
        d_scores = probs * (d_probs - jnp.sum(probs * d_probs, axis=1, keepdims=True))
        d_low = (d_scores * factor).astype(BF16)
        d_keys.append(dot(d_low, q2, TN))
        d_values.append(dot(probs_low, da2, TN))
    d_kv = jnp.concatenate(d_keys + d_values, axis=1).astype(BF16)
    pass_on(1)

    inner = [jnp.zeros((128, 256), F32)]

    def memory_chunk(x_, j):
        v = dot(d_kv, weight_rows(x_, j, slice(256, 768)), NT)
        inner[0] = inner[0] + v * (act[0, x_, j].astype(F32) * aux[x_, j, 0:1, :])
        return v

    hand_out(0, memory_chunk)
    own_inner = as_row(jnp.sum(inner[0], axis=1, keepdims=True))
    stat_out[0:1, :] = own_inner
    stat_out[1:8, :] = jnp.zeros((7, 128), F32)
    for i, to in enumerate((right, left, across)):
        send(stat_out, stat_in.at[i], S_STAT + i, to)
    pass_on(0)

    cross = [
        copy(last.at[other, zh], last_in.at[0], F_SUM, r1),
        copy(last.at[other, oh], last_in.at[2], F_SUM + 2, r3),
    ]
    same = copy(last.at[side, oh], last_in.at[1], F_SUM + 1, r2)

    def to_owner(kind):
        @pl.when(side == kind)
        def _():
            same.start()

        @pl.when(side != kind)
        def _():
            for one in cross:
                one.start()

    finish(1)
    to_owner(1)
    for i in range(3):
        arrived(stat_in.at[i], S_STAT + i)
    part_inner = own_inner
    for i in range(3):
        part_inner = part_inner + stat_in[i, 0:1, :]
    part_inner = part_inner + jnp.where(zh == 0, c_inner, 0.0)
    last_stat[0:1, :] = part_inner
    last_stat[1:2, :] = as_row(inv_e)
    last_stat[2:8, :] = jnp.zeros((6, 128), F32)
    for i, to in enumerate((r1, r2, r3)):
        send(last_stat, stat_last.at[i], F_STAT + i, to)
    finish(0)
    to_owner(0)

    for i in range(3):
        arrived(stat_last.at[i], F_STAT + i)
        arrived(last_in.at[i], F_SUM + i)
    sums = (
        hold[side, 2 + zh] + last_in[1].astype(F32),
        last_in[0].astype(F32) + last_in[2].astype(F32),
    )

    @pl.when(side == 1)
    def _():
        for m, total in ((1, sums[0]), (0, sums[1])):
            out[m] = (rows[m].astype(F32) + total).astype(BF16)

    @pl.when(side == 0)
    def _():
        inners = (
            part_inner + stat_last[1, 0:1, :],
            stat_last[0, 0:1, :] + stat_last[2, 0:1, :],
        )
        invs = (inv_e, as_col(stat_last[0, 1:2, :]))
        for m in range(2):
            weighted = (sums[m] + cot[m].astype(F32)) * mgain[...]
            mean = as_col(inners[m]) / D
            inv = invs[m]
            d_rows = inv * weighted - rows[m].astype(F32) * (inv * inv * inv * mean)
            out[m] = d_rows.astype(BF16)

    for one in pending:
        one.wait_send()
    same.wait_send()
    for one in cross:
        one.wait_send()

    @pl.when(side == 1)
    def _():
        for one in cots:
            one.wait_send()

    @pl.when(side == 0)
    def _():
        for one in auxes:
            one.wait_send()


def local(segment_rows, row_cotangent, memory_gain, cross_gain, w_query, w_key, w_value, w_out):
    vmem = pl.BlockSpec(memory_space=pltpu.VMEM)
    return pl.pallas_call(
        kernel,
        out_shape=jax.ShapeDtypeStruct((2, 128, 256), BF16),
        in_specs=[vmem] * 8,
        out_specs=vmem,
        scratch_shapes=[
            pltpu.VMEM((4, NY, 2, 32, 1024), BF16),
            pltpu.VMEM((3, NX, 2, 128, 256), BF16),
            pltpu.VMEM((NX, 2, 8, 256), F32),
            pltpu.VMEM((2, 4, 128, 256), F32),
            pltpu.VMEM((2, 6, 128, 256), BF16),
            pltpu.VMEM((2, 4, 128, 256), BF16),
            pltpu.VMEM((2, 2, 128, 256), BF16),
            pltpu.VMEM((8, 128), F32),
            pltpu.VMEM((3, 8, 128), F32),
            pltpu.VMEM((2, 2, 128, 256), BF16),
            pltpu.VMEM((3, 128, 256), BF16),
            pltpu.VMEM((8, 128), F32),
            pltpu.VMEM((3, 8, 128), F32),
            pltpu.SemaphoreType.DMA((COPIES,)),
            pltpu.SemaphoreType.DMA((COPIES,)),
        ],
        compiler_params=pltpu.CompilerParams(
            collective_id=0, has_side_effects=True, vmem_limit_bytes=48 * 1024 * 1024
        ),
    )(
        segment_rows, row_cotangent, memory_gain.reshape(1, -1), cross_gain.reshape(1, -1),
        w_query, w_key, w_value, w_out,
    )


def solution(mesh):
    in_specs = (
        P(None, "segment", "head"),
        P(None, "segment", "head"),
        P("head"),
        P("head"),
        P("segment", "head"),
        P("segment", "head"),
        P("segment", "head"),
        P("head", "segment"),
    )
    out_specs = P(None, "segment", "head")
    return jax.shard_map(local, mesh=mesh, in_specs=in_specs, out_specs=out_specs, check_vma=False)
```

```python
import functools

import jax
import jax.numpy as jnp
from jax import lax
from jax.experimental import pallas as pl
from jax.experimental.pallas import tpu as pltpu
from jax.sharding import PartitionSpec as P

D = 2048
HS = 64
EPS = 1e-06
NX = 4
NY = 8
NT = (((1,), (1,)), ((), ()))
TN = (((0,), (0,)), ((), ()))
F32 = jnp.float32
BF16 = jnp.bfloat16

Q_Z = 0
Q_UP = 3
Q_DOWN = 19
Q_MATE = 35
O_Z = 43
O_UP = 46
O_DOWN = 50
O_MATE = 54
A_ROWS = 62
A_COT = 65
A_AUX = 68
X_ROWS = 71
X_COT = 83
X_AUX = 95
S_OUT = 98
S_STAT = 110
F_SUM = 113
F_STAT = 116
COPIES = 119


def dot(a, b, dims=(((1,), (0,)), ((), ()))):
    return lax.dot_general(a, b, dims, preferred_element_type=F32)


def kernel(
    rows_h, cot_h, mgain_h, cgain_h, wq, wk, wv, wo, out,
    rows, cot, gains, wa, wb, act, aux, hold, stage, near, far, stat_out, stat_in, last, last_in, last_stat,
    stat_last, lsem, ssem, rsem,
):
    seg = lax.axis_index("segment")
    head = lax.axis_index("head")
    c = seg % 2
    y = (seg // 2) % NY
    zl = seg // (2 * NY)
    p = zl % 2
    side = zl // 2
    x = head // 2
    zh = head % 2
    oh = 1 - zh
    other = 1 - side

    def at(x_=x, y_=y, zl_=zl, zh_=zh, c_=c):
        return ((zl_ * NY + y_) * 2 + c_, x_ * 2 + zh_)

    xr, xl, xx = (x + 1) % NX, (x + NX - 1) % NX, (x + 2) % NX
    right, left, across = at(x_=xr), at(x_=xl), at(x_=xx)
    up, down = at(y_=(y + 1) % NY), at(y_=(y + NY - 1) % NY)
    mate = at(c_=1 - c)
    zl_of = (zl, (1 - p) + 2 * side, p + 2 * other, (1 - p) + 2 * other)
    w_to = [None] + [at(zl_=v) for v in zl_of[1:]]
    r1, r2, r3 = at(zl_=zl_of[2]), at(zh_=oh), at(zl_=zl_of[2], zh_=oh)

    def copy(src, dst, number, to):
        return pltpu.make_async_remote_copy(
            src_ref=src, dst_ref=dst, send_sem=ssem.at[number], recv_sem=rsem.at[number],
            device_id=to, device_id_type=pl.DeviceIdType.MESH,
        )

    pending = []

    def send(src, dst, number, to):
        one = copy(src, dst, number, to)
        one.start()
        pending.append(one)

    def arrived(dst, number):
        copy(dst, dst, number, mate).wait_recv()

    eye = lax.broadcasted_iota(jnp.int32, (128, 128), 0) == lax.broadcasted_iota(
        jnp.int32, (128, 128), 1
    )

    def as_row(col):
        return jnp.sum(jnp.where(eye, col, 0.0), axis=0, keepdims=True)

    def as_col(row):
        return jnp.sum(jnp.where(eye, row, 0.0), axis=1, keepdims=True)

    barrier = pltpu.get_barrier_semaphore()
    partners = (right, left, across, up, down, mate, r1, r2, r3, w_to[1], w_to[3])
    for partner in partners:
        pl.semaphore_signal(
            barrier, inc=1, device_id=partner, device_id_type=pl.DeviceIdType.MESH
        )
    own, own_o = wa.at[zl, y, c], wb.at[zl, y, c]
    places = [(ref, own.at[:, 256 * i : 256 * i + 256]) for i, ref in enumerate((wq, wk, wv))]
    places += [(wo, own_o), (rows_h, rows), (cot_h, cot)]
    places += [(mgain_h, gains.at[0]), (cgain_h, gains.at[1]), (rows_h.at[side], act.at[side, x, zh])]
    fetch = [
        pltpu.make_async_copy(src, dst, lsem.at[i]) for i, (src, dst) in enumerate(places)
    ]
    fetch_cot = pltpu.make_async_copy(cot_h.at[1], act.at[2, x, zh], lsem.at[len(fetch)])
    for one in fetch:
        one.start()
    encoder, decoder = side == 0, side == 1

    @pl.when(decoder)
    def _():
        fetch_cot.start()

    for one in fetch[:4]:
        one.wait()
    pl.semaphore_wait(barrier, len(partners))

    waits = {0: [], 1: []}

    def send_when(of_side, copies):
        @pl.when(side == of_side)
        def _():
            for one in copies:
                one.start()

        waits[of_side].extend(copies)

    def ring_block(t, d):
        return wa.at[zl_of[d], (y + NY + t) % NY, c]

    def forward(t, d):
        if 0 < t < 4 or (t == 4 and d < 2):
            arrived(ring_block(-t, d), Q_UP + 4 * (t - 1) + d)
        if t < 3 or (t == 3 and d < 2):
            send(ring_block(-t, d), ring_block(-t, d), Q_UP + 4 * t + d, up)
        if 0 < t < 4 or (t == 4 and d >= 2):
            arrived(ring_block(t, d), Q_DOWN + 4 * (t - 1) + d)
        if t < 3 or (t == 3 and d >= 2):
            send(ring_block(t, d), ring_block(t, d), Q_DOWN + 4 * t + d, down)

    def from_z(d):
        arrived(ring_block(0, d), Q_Z + d - 1)
        forward(0, d)

    def share(t):
        block = wa.at[:, (y + NY + t) % NY, c]
        send(block, block, Q_MATE + t % NY, mate)

    def out_block(t, half=None):
        parts = slice(0, 4) if half is None else slice(2 * half, 2 * half + 2)
        return wb.at[parts, (y + NY + t) % NY, c]

    def forward_out(t):
        half = (0, 1) if t >= 3 else (None, None)
        took = (0, 1) if t == 4 else (None, None)
        for step, number, to, i in ((-t, O_UP, up, 0), (t, O_DOWN, down, 1)):
            if t > 0:
                arrived(out_block(step, took[i]), number + t - 1)
            if t < 4:
                block = out_block(step, half[i])
                send(block, block, number + t, to)

    def share_out(t):
        block = wb.at[:, (y + NY + t) % NY, c]
        send(block, block, O_MATE + t % NY, mate)

    peers = (right, left, across)
    z_peers = ((r1, other), (r2, side), (r3, other))
    mine, my_cot, my_aux = act.at[side, x, zh], act.at[2, x, zh], aux.at[x, zh]
    kinds = (side, other, side, other)
    z_of = (zh, zh, oh, oh)
    cot_side = (1, 0, 1, 0)
    ring = (xl, xr, xx)

    def rows_block(s, x_):
        return act.at[kinds[s], x_, z_of[s]]

    def cot_block(s, x_):
        return act.at[2, x_, z_of[s]]

    def rows_arrived(s, i):
        arrived(rows_block(s, ring[i]), X_ROWS + 3 * s + i)

    def cot_arrived(s, i):
        @pl.when(side == cot_side[s])
        def _():
            arrived(cot_block(s, ring[i]), X_COT + 3 * s + i)

    def rows_along_x(s):
        block = rows_block(s, x)
        arrived(block, A_ROWS + s - 1)
        for i in range(2):
            send(block, block, X_ROWS + 3 * s + i, peers[i])

    def cot_along_x(s):
        block = cot_block(s, x)

        @pl.when(side == cot_side[s])
        def _():
            arrived(block, A_COT + s - 1)

        send_when(cot_side[s], [copy(block, block, X_COT + 3 * s + i, peers[i]) for i in range(2)])

    def rows_relay(s):
        i = 1 if s == 3 else 0
        rows_arrived(s, i)
        block = rows_block(s, ring[i])
        send(block, block, X_ROWS + 3 * s + 2, peers[i])

    def cot_relay(s):
        i = 0 if s == 3 else 1
        cot_arrived(s, i)
        block = cot_block(s, ring[i])
        send_when(cot_side[s], [copy(block, block, X_COT + 3 * s + 2, peers[i])])

    def make_aux():
        for one in fetch[4:]:
            one.wait()

        @pl.when(decoder)
        def _():
            fetch_cot.wait()

        @pl.when(encoder)
        def _():
            aux[x, zh, 0:1, :] = gains[0]
            aux[x, zh, 1:2, :] = gains[1]
            for m in range(2):
                inner = rows[m].astype(F32) * cot[m].astype(F32) * gains[0]
                aux[x, zh, 2:3, 128 * m : 128 * m + 128] = as_row(
                    jnp.sum(inner, axis=1, keepdims=True)
                )
            aux[x, zh, 3:8, :] = jnp.zeros((5, 256), F32)

        send_when(0, [copy(my_aux, my_aux, A_AUX + i, to) for i, to in enumerate((r1, r2, r3))])

    def aux_along_x():
        @pl.when(encoder)
        def _():
            arrived(aux.at[x, oh], A_AUX + 1)

        @pl.when(decoder)
        def _():
            arrived(aux.at[x, zh], A_AUX)
            arrived(aux.at[x, oh], A_AUX + 2)

        for i, to in enumerate(peers):
            send(aux.at[x], aux.at[x], X_AUX + i, to)

    forward(0, 0)
    for d in (1, 2, 3):
        send(own, own, Q_Z + d - 1, w_to[d])
    for i, to in enumerate(peers):
        send(rows_h.at[side], mine, X_ROWS + i, to)
    send_when(1, [copy(cot_h.at[1], my_cot, X_COT + i, to) for i, to in enumerate(peers)])
    forward(1, 0)
    for d in (1, 2, 3):
        send(own_o, own_o, O_Z + d - 1, w_to[d])
    from_z(1)
    forward(2, 0)
    from_z(2)
    from_z(3)
    for i in (0, 2, 1):
        to, m = z_peers[i]
        send(rows_h.at[m], mine, A_ROWS + i, to)
    make_aux()
    share(0)
    forward(3, 0)
    for d in (1, 2, 3):
        forward(1, d)
    share(1)
    share(-1)
    for d in (1, 2, 3):
        arrived(wb.at[zl_of[d], y, c], O_Z + d - 1)
    forward_out(0)
    send_when(1, [copy(cot_h.at[z_peers[i][1]], my_cot, A_COT + i, z_peers[i][0]) for i in (0, 2, 1)])
    for d in (1, 2, 3):
        forward(2, d)
    share(2)
    share(-2)
    rows_along_x(1)
    rows_along_x(3)
    aux_along_x()
    forward_out(1)
    rows_along_x(2)
    for d in (1, 2, 3):
        forward(3, d)
    share(3)
    share(-3)
    rows_relay(1)
    rows_relay(3)
    forward_out(2)
    for s in (1, 3, 2):
        cot_along_x(s)
    rows_relay(2)
    for d in range(4):
        forward(4, d)
    share(4)
    forward_out(3)
    for s in (1, 3, 2):
        cot_relay(s)
    for t in (0, 1, -1, 2, -2, 3, -3):
        share_out(t)
    forward_out(4)
    share_out(4)

    for i in range(3):
        rows_arrived(0, i)
        arrived(aux.at[ring[i]], X_AUX + i)
    for s, first in ((1, 0), (2, 0), (3, 1)):
        rows_arrived(s, 1 - first)
        rows_arrived(s, 2)
    for t in range(NY):
        arrived(wa.at[:, (y + t) % NY, 1 - c], Q_MATE + t)

    blocks = [(i // 2, i % 2) for i in range(8)]

    def inverse(kind):
        total = jnp.zeros((128, 256), F32)
        for i, j in blocks:
            v = act[kind, i, j].astype(F32)
            total = total + v * v
        return lax.rsqrt(jnp.sum(total, axis=1, keepdims=True) / D + EPS)

    inv_e = inverse(0)
    inv_x = inverse(1)
    kv = jnp.zeros((128, 512), F32)
    q = jnp.zeros((128, 256), F32)
    c_inner = jnp.zeros((1, 256), F32)
    for i, j in blocks:
        memory = (act[0, i, j].astype(F32) * inv_e * aux[i, j, 0:1, :]).astype(BF16)
        normed = (act[1, i, j].astype(F32) * inv_x * aux[i, j, 1:2, :]).astype(BF16)
        part = wa.at[i, 4 * j : 4 * j + 4]
        kv = kv + dot(memory, part[:, :, :, 256:768].reshape(256, 512))
        q = q + dot(normed, part[:, :, :, 0:256].reshape(256, 256))
        c_inner = c_inner + aux[i, j, 2:3, :]
    kv = kv.astype(BF16).astype(F32)
    q = q.astype(BF16).astype(F32)
    c_inner = jnp.where(side == 0, c_inner[:, 0:128], c_inner[:, 128:256])

    low = lax.broadcasted_iota(jnp.int32, (128, 128), 1) < HS
    factor = HS ** (-0.5)

    def two(v):
        return jnp.concatenate(
            [jnp.where(low, v, 0.0).astype(BF16), jnp.where(low, 0.0, v).astype(BF16)], axis=0
        )

    attended, saved = [], []
    for pair in range(2):
        lanes = slice(128 * pair, 128 * pair + 128)
        q2 = two(q[:, lanes])
        key = kv[:, lanes].astype(BF16)
        value = kv[:, 256 + 128 * pair : 384 + 128 * pair]
        scores = dot(q2, key, NT) * factor
        e = jnp.exp(scores - jnp.max(scores, axis=1, keepdims=True))
        probs = e / jnp.sum(e, axis=1, keepdims=True)
        probs_low = probs.astype(BF16)
        v2 = two(value)
        attended.append(dot(probs_low[:128], v2[:128]) + dot(probs_low[128:], v2[128:]))
        saved.append((q2, value.astype(BF16), probs, probs_low))
    attended = jnp.concatenate(attended, axis=1).astype(BF16)

    for t in range(NY):
        arrived(wb.at[:, (y + t) % NY, 1 - c], O_MATE + t)

    def hand_out(kind, chunk):
        base = S_OUT + 6 * kind
        for i, (x_, z_, to, dst) in enumerate(
            (
                (xx, oh, right, far.at[kind, 0]),
                (xx, zh, left, far.at[kind, 1]),
                (xr, zh, right, near.at[kind, 0]),
                (xl, oh, left, near.at[kind, 1]),
            )
        ):
            stage[kind, i] = chunk(x_, z_).astype(BF16)
            send(stage.at[kind, i], dst, base + i, to)
        for i, (x_, z_) in enumerate(((xr, oh), (xl, zh), (x, oh), (x, zh))):
            hold[kind, i] = chunk(x_, z_)

    def pass_on(kind):
        base = S_OUT + 6 * kind
        for i, to in enumerate((right, left)):
            arrived(far.at[kind, i], base + i)
            stage[kind, 4 + i] = (hold[kind, i] + far[kind, i].astype(F32)).astype(BF16)
            send(stage.at[kind, 4 + i], near.at[kind, 2 + i], base + 4 + i, to)

    def finish(kind):
        base = S_OUT + 6 * kind
        for j, pair in enumerate(((1, 2), (0, 3))):
            total = hold[kind, 2 + j]
            for i in pair:
                arrived(near.at[kind, i], base + 2 + i)
                total = total + near[kind, i].astype(F32)
            hold[kind, 2 + j] = total
            last[kind, j] = total.astype(BF16)
            if j == 0:
                slot = 2 - side if kind else 1 + side
                send(
                    last.at[kind, 0], last_in.at[slot], F_SUM + slot,
                    at(zl_=p + 2 * kind, zh_=oh),
                )
            else:
                send_when(1 - kind, [copy(last.at[kind, 1], last_in.at[0], F_SUM, r1)])

    hand_out(1, lambda x_, j: dot(attended, wb[x_, pl.ds(4 * j, 4)].reshape(256, 256), NT))

    for i in range(3):
        cot_arrived(0, i)
    for s, first in ((1, 1), (2, 1), (3, 0)):
        cot_arrived(s, 1 - first)
        cot_arrived(s, 2)
    da = jnp.zeros((128, 256), F32)
    for i, j in blocks:
        da = da + dot(act[2, i, j], wb[i, 4 * j : 4 * j + 4].reshape(256, 256))
    da = da.astype(BF16).astype(F32)

    d_keys, d_values = [], []
    for pair, (q2, value, probs, probs_low) in enumerate(saved):
        da2 = two(da[:, 128 * pair : 128 * pair + 128])
        d_probs = dot(da2, value, NT)
        d_scores = probs * (d_probs - jnp.sum(probs * d_probs, axis=1, keepdims=True))
        d_low = (d_scores * factor).astype(BF16)
        d_keys.append(dot(d_low, q2, TN))
        d_values.append(dot(probs_low, da2, TN))
    d_kv = jnp.concatenate(d_keys + d_values, axis=1).astype(BF16)
    pass_on(1)
    inner = [jnp.zeros((128, 256), F32)]

    def memory_chunk(x_, j):
        v = dot(d_kv, wa[x_, pl.ds(4 * j, 4), :, :, 256:768].reshape(256, 512), NT)
        inner[0] = inner[0] + v * (act[0, x_, j].astype(F32) * aux[x_, j, 0:1, :])
        return v

    hand_out(0, memory_chunk)
    own_inner = as_row(jnp.sum(inner[0], axis=1, keepdims=True))
    stat_out[0:1, :] = own_inner
    stat_out[1:8, :] = jnp.zeros((7, 128), F32)
    for i, to in enumerate((right, left, across)):
        send(stat_out, stat_in.at[i], S_STAT + i, to)
    pass_on(0)

    finish(1)
    for i in range(3):
        arrived(stat_in.at[i], S_STAT + i)
    part_inner = own_inner
    for i in range(3):
        part_inner = part_inner + stat_in[i, 0:1, :]
    part_inner = part_inner + jnp.where(zh == 0, c_inner, 0.0)
    last_stat[0:1, :] = part_inner
    last_stat[1:2, :] = as_row(inv_e)
    last_stat[2:8, :] = jnp.zeros((6, 128), F32)
    for i, to in enumerate((r1, r2, r3)):
        send(last_stat, stat_last.at[i], F_STAT + i, to)
    finish(0)

    for i in range(3):
        arrived(stat_last.at[i], F_STAT + i)
        arrived(last_in.at[i], F_SUM + i)
    sums = (
        hold[side, 3] + last_in[1].astype(F32),
        last_in[0].astype(F32) + last_in[2].astype(F32),
    )

    @pl.when(side == 1)
    def _():
        for m, total in ((1, sums[0]), (0, sums[1])):
            out[m] = (rows[m].astype(F32) + total).astype(BF16)

    @pl.when(side == 0)
    def _():
        inners = (
            part_inner + stat_last[1, 0:1, :],
            stat_last[0, 0:1, :] + stat_last[2, 0:1, :],
        )
        invs = (inv_e, as_col(stat_last[0, 1:2, :]))
        for m in range(2):
            weighted = (sums[m] + cot[m].astype(F32)) * gains[0]
            mean = as_col(inners[m]) / D
            inv = invs[m]
            d_rows = inv * weighted - rows[m].astype(F32) * (inv * inv * inv * mean)
            out[m] = d_rows.astype(BF16)

    for one in pending:
        one.wait_send()
    for of_side in (0, 1):

        @pl.when(side == of_side)
        def _(of_side=of_side):
            for one in waits[of_side]:
                one.wait_send()


def local(segment_rows, row_cotangent, memory_gain, cross_gain, w_query, w_key, w_value, w_out):
    return pl.pallas_call(
        kernel,
        out_shape=jax.ShapeDtypeStruct((2, 128, 256), BF16),
        in_specs=[pl.BlockSpec(memory_space=pl.ANY)] * 8,
        out_specs=pl.BlockSpec(memory_space=pltpu.VMEM),
        scratch_shapes=[
            pltpu.VMEM((2, 128, 256), BF16),
            pltpu.VMEM((2, 128, 256), BF16),
            pltpu.VMEM((2, 1, 256), F32),
            pltpu.VMEM((4, NY, 2, 32, 768), BF16),
            pltpu.VMEM((4, NY, 2, 32, 256), BF16),
            pltpu.VMEM((3, NX, 2, 128, 256), BF16),
            pltpu.VMEM((NX, 2, 8, 256), F32),
            pltpu.VMEM((2, 4, 128, 256), F32),
            pltpu.VMEM((2, 6, 128, 256), BF16),
            pltpu.VMEM((2, 4, 128, 256), BF16),
            pltpu.VMEM((2, 2, 128, 256), BF16),
            pltpu.VMEM((8, 128), F32),
            pltpu.VMEM((3, 8, 128), F32),
            pltpu.VMEM((2, 2, 128, 256), BF16),
            pltpu.VMEM((3, 128, 256), BF16),
            pltpu.VMEM((8, 128), F32),
            pltpu.VMEM((3, 8, 128), F32),
            pltpu.SemaphoreType.DMA((10,)),
            pltpu.SemaphoreType.DMA((COPIES,)),
            pltpu.SemaphoreType.DMA((COPIES,)),
        ],
        compiler_params=pltpu.CompilerParams(
            collective_id=0, has_side_effects=True, vmem_limit_bytes=60 * 1024 * 1024
        ),
    )(
        segment_rows, row_cotangent, memory_gain.reshape(1, -1), cross_gain.reshape(1, -1),
        w_query, w_key, w_value, w_out.T,
    )


def solution(mesh):
    in_specs = (
        P(None, "segment", "head"),
        P(None, "segment", "head"),
        P("head"),
        P("head"),
        P("segment", "head"),
        P("segment", "head"),
        P("segment", "head"),
        P("head", "segment"),
    )
    out_specs = P(None, "segment", "head")
    return jax.shard_map(local, mesh=mesh, in_specs=in_specs, out_specs=out_specs, check_vma=False)
```

```python
import functools

import jax
import jax.numpy as jnp
from jax import lax
from jax.experimental import pallas as pl
from jax.experimental.pallas import tpu as pltpu
from jax.sharding import PartitionSpec as P

D = 2048
HS = 64
EPS = 1e-06
NX = 4
NY = 8
NT = (((1,), (1,)), ((), ()))
TN = (((0,), (0,)), ((), ()))
F32 = jnp.float32
BF16 = jnp.bfloat16

W_Z = 0
W_UP = 3
W_DOWN = 19
W_MATE = 35
W_LAST = 43
A_ROWS = 47
A_COT = 50
A_AUX = 53
X_ROWS = 56
X_COT = 68
X_AUX = 80
S_OUT = 83
S_STAT = 95
F_SUM = 98
F_STAT = 101
COPIES = 104


def dot(a, b, dims=(((1,), (0,)), ((), ()))):
    return lax.dot_general(a, b, dims, preferred_element_type=F32)


def kernel(
    rows_h, cot_h, mgain_h, cgain_h, wq, wk, wv, wo, out,
    rows, cot, gains, w, act, aux, hold, stage, near, far, stat_out, stat_in, last, last_in, last_stat,
    stat_last, lsem, ssem, rsem,
):
    seg = lax.axis_index("segment")
    head = lax.axis_index("head")
    c = seg % 2
    y = (seg // 2) % NY
    zl = seg // (2 * NY)
    p = zl % 2
    side = zl // 2
    x = head // 2
    zh = head % 2
    oh = 1 - zh
    other = 1 - side

    def at(x_=x, y_=y, zl_=zl, zh_=zh, c_=c):
        return ((zl_ * NY + y_) * 2 + c_, x_ * 2 + zh_)

    xr, xl, xx = (x + 1) % NX, (x + NX - 1) % NX, (x + 2) % NX
    right, left, across = at(x_=xr), at(x_=xl), at(x_=xx)
    up, down = at(y_=(y + 1) % NY), at(y_=(y + NY - 1) % NY)
    mate = at(c_=1 - c)
    zl_of = (zl, (1 - p) + 2 * side, p + 2 * other, (1 - p) + 2 * other)
    w_to = [None] + [at(zl_=v) for v in zl_of[1:]]
    r1, r2, r3 = at(zl_=zl_of[2]), at(zh_=oh), at(zl_=zl_of[2], zh_=oh)

    def copy(src, dst, number, to):
        return pltpu.make_async_remote_copy(
            src_ref=src, dst_ref=dst, send_sem=ssem.at[number], recv_sem=rsem.at[number],
            device_id=to, device_id_type=pl.DeviceIdType.MESH,
        )

    pending = []

    def send(src, dst, number, to):
        one = copy(src, dst, number, to)
        one.start()
        pending.append(one)

    def arrived(dst, number):
        copy(dst, dst, number, mate).wait_recv()

    eye = lax.broadcasted_iota(jnp.int32, (128, 128), 0) == lax.broadcasted_iota(
        jnp.int32, (128, 128), 1
    )

    def as_row(col):
        return jnp.sum(jnp.where(eye, col, 0.0), axis=0, keepdims=True)

    def as_col(row):
        return jnp.sum(jnp.where(eye, row, 0.0), axis=1, keepdims=True)

    barrier = pltpu.get_barrier_semaphore()
    partners = (right, left, across, up, down, mate, r1, r2, r3, w_to[1], w_to[3])
    for partner in partners:
        pl.semaphore_signal(
            barrier, inc=1, device_id=partner, device_id_type=pl.DeviceIdType.MESH
        )
    own = w.at[zl, y, c]
    places = [(ref, own.at[:, 256 * i : 256 * i + 256]) for i, ref in enumerate((wq, wk, wv, wo))]
    places += [(rows_h, rows), (cot_h, cot)]
    places += [(mgain_h, gains.at[0]), (cgain_h, gains.at[1]), (rows_h.at[side], act.at[side, x, zh])]
    fetch = [
        pltpu.make_async_copy(src, dst, lsem.at[i]) for i, (src, dst) in enumerate(places)
    ]
    fetch_cot = pltpu.make_async_copy(cot_h.at[1], act.at[2, x, zh], lsem.at[len(fetch)])
    for one in fetch:
        one.start()
    encoder, decoder = side == 0, side == 1

    @pl.when(decoder)
    def _():
        fetch_cot.start()

    for one in fetch[:4]:
        one.wait()
    pl.semaphore_wait(barrier, len(partners))

    waits = {0: [], 1: []}

    def send_when(of_side, copies):
        @pl.when(side == of_side)
        def _():
            for one in copies:
                one.start()

        waits[of_side].extend(copies)

    def ring_block(t, d):
        return w.at[zl_of[d], (y + NY + t) % NY, c]

    def forward(t, d):
        if 0 < t < 4 or (t == 4 and d < 2):
            arrived(ring_block(-t, d), W_UP + 4 * (t - 1) + d)
        if t < 3 or (t == 3 and d < 2):
            send(ring_block(-t, d), ring_block(-t, d), W_UP + 4 * t + d, up)
        if 0 < t < 4 or (t == 4 and d >= 2):
            arrived(ring_block(t, d), W_DOWN + 4 * (t - 1) + d)
        if t < 3 or (t == 3 and d >= 2):
            send(ring_block(t, d), ring_block(t, d), W_DOWN + 4 * t + d, down)

    def from_z(d):
        arrived(ring_block(0, d), W_Z + d - 1)
        forward(0, d)

    def share(t):
        block = w.at[:, (y + NY + t) % NY, c]
        send(block, block, W_MATE + t % NY, mate)

    def share_block(t, d):
        block = ring_block(t, d)
        send(block, block, W_LAST + d, mate)

    peers = (right, left, across)
    z_peers = ((r1, other), (r2, side), (r3, other))
    mine, my_cot, my_aux = act.at[side, x, zh], act.at[2, x, zh], aux.at[x, zh]
    kinds = (side, other, side, other)
    z_of = (zh, zh, oh, oh)
    cot_side = (1, 0, 1, 0)
    ring = (xl, xr, xx)

    def rows_block(s, x_):
        return act.at[kinds[s], x_, z_of[s]]

    def cot_block(s, x_):
        return act.at[2, x_, z_of[s]]

    def rows_arrived(s, i):
        arrived(rows_block(s, ring[i]), X_ROWS + 3 * s + i)

    def cot_arrived(s, i):
        @pl.when(side == cot_side[s])
        def _():
            arrived(cot_block(s, ring[i]), X_COT + 3 * s + i)

    def rows_along_x(s):
        block = rows_block(s, x)
        arrived(block, A_ROWS + s - 1)
        for i in range(2):
            send(block, block, X_ROWS + 3 * s + i, peers[i])

    def cot_along_x(s):
        block = cot_block(s, x)

        @pl.when(side == cot_side[s])
        def _():
            arrived(block, A_COT + s - 1)

        send_when(cot_side[s], [copy(block, block, X_COT + 3 * s + i, peers[i]) for i in range(2)])

    def rows_relay(s):
        i = 1 if s == 3 else 0
        rows_arrived(s, i)
        block = rows_block(s, ring[i])
        send(block, block, X_ROWS + 3 * s + 2, peers[i])

    def cot_relay(s):
        i = 0 if s == 3 else 1
        cot_arrived(s, i)
        block = cot_block(s, ring[i])
        send_when(cot_side[s], [copy(block, block, X_COT + 3 * s + 2, peers[i])])

    def make_aux():
        for one in fetch[4:]:
            one.wait()

        @pl.when(decoder)
        def _():
            fetch_cot.wait()

        @pl.when(encoder)
        def _():
            aux[x, zh, 0:1, :] = gains[0]
            aux[x, zh, 1:2, :] = gains[1]
            for m in range(2):
                inner = rows[m].astype(F32) * cot[m].astype(F32) * gains[0]
                aux[x, zh, 2:3, 128 * m : 128 * m + 128] = as_row(
                    jnp.sum(inner, axis=1, keepdims=True)
                )
            aux[x, zh, 3:8, :] = jnp.zeros((5, 256), F32)

        send_when(0, [copy(my_aux, my_aux, A_AUX + i, to) for i, to in enumerate((r1, r2, r3))])

    def aux_along_x():
        @pl.when(encoder)
        def _():
            arrived(aux.at[x, oh], A_AUX + 1)

        @pl.when(decoder)
        def _():
            arrived(aux.at[x, zh], A_AUX)
            arrived(aux.at[x, oh], A_AUX + 2)

        for i, to in enumerate(peers):
            send(aux.at[x], aux.at[x], X_AUX + i, to)

    forward(0, 0)
    for d in (1, 2, 3):
        send(own, own, W_Z + d - 1, w_to[d])
    for i, to in enumerate(peers):
        send(rows_h.at[side], mine, X_ROWS + i, to)
    send_when(1, [copy(cot_h.at[1], my_cot, X_COT + i, to) for i, to in enumerate(peers)])
    from_z(1)
    from_z(2)
    from_z(3)
    for i in (0, 2, 1):
        to, m = z_peers[i]
        send(rows_h.at[m], mine, A_ROWS + i, to)
    make_aux()
    send_when(1, [copy(cot_h.at[z_peers[i][1]], my_cot, A_COT + i, z_peers[i][0]) for i in (0, 2, 1)])
    share(0)
    forward(1, 0)
    forward(1, 1)
    forward(1, 2)
    forward(1, 3)
    share(1)
    share(-1)
    forward(2, 0)
    forward(2, 1)
    forward(2, 2)
    forward(2, 3)
    share(2)
    share(-2)
    rows_along_x(1)
    rows_along_x(3)
    aux_along_x()
    rows_along_x(2)
    forward(3, 0)
    forward(3, 1)
    forward(3, 2)
    forward(3, 3)
    share(3)
    share(-3)
    rows_relay(1)
    rows_relay(3)
    for s in (1, 3, 2):
        cot_along_x(s)
    rows_relay(2)
    for d in range(4):
        forward(4, d)
        share_block(4, d)
    for s in (1, 3, 2):
        cot_relay(s)

    for i in range(3):
        rows_arrived(0, i)
        arrived(aux.at[ring[i]], X_AUX + i)
    for s, first in ((1, 0), (2, 0), (3, 1)):
        rows_arrived(s, 1 - first)
        rows_arrived(s, 2)
    for t in range(NY):
        if t == 4:
            for d in range(4):
                arrived(w.at[zl_of[d], (y + 4) % NY, 1 - c], W_LAST + d)
        else:
            arrived(w.at[:, (y + t) % NY, 1 - c], W_MATE + t)

    blocks = [(i // 2, i % 2) for i in range(8)]

    def inverse(kind):
        total = jnp.zeros((128, 256), F32)
        for i, j in blocks:
            v = act[kind, i, j].astype(F32)
            total = total + v * v
        return lax.rsqrt(jnp.sum(total, axis=1, keepdims=True) / D + EPS)

    inv_e = inverse(0)
    inv_x = inverse(1)
    kv = jnp.zeros((128, 512), F32)
    q = jnp.zeros((128, 256), F32)
    c_inner = jnp.zeros((1, 256), F32)
    for i, j in blocks:
        memory = (act[0, i, j].astype(F32) * inv_e * aux[i, j, 0:1, :]).astype(BF16)
        normed = (act[1, i, j].astype(F32) * inv_x * aux[i, j, 1:2, :]).astype(BF16)
        part = w.at[i, 4 * j : 4 * j + 4]
        kv = kv + dot(memory, part[:, :, :, 256:768].reshape(256, 512))
        q = q + dot(normed, part[:, :, :, 0:256].reshape(256, 256))
        c_inner = c_inner + aux[i, j, 2:3, :]
    kv = kv.astype(BF16).astype(F32)
    q = q.astype(BF16).astype(F32)
    c_inner = jnp.where(side == 0, c_inner[:, 0:128], c_inner[:, 128:256])

    low = lax.broadcasted_iota(jnp.int32, (128, 128), 1) < HS
    factor = HS ** (-0.5)

    def two(v):
        return jnp.concatenate(
            [jnp.where(low, v, 0.0).astype(BF16), jnp.where(low, 0.0, v).astype(BF16)], axis=0
        )

    attended, saved = [], []
    for pair in range(2):
        lanes = slice(128 * pair, 128 * pair + 128)
        q2 = two(q[:, lanes])
        key = kv[:, lanes].astype(BF16)
        value = kv[:, 256 + 128 * pair : 384 + 128 * pair]
        scores = dot(q2, key, NT) * factor
        e = jnp.exp(scores - jnp.max(scores, axis=1, keepdims=True))
        probs = e / jnp.sum(e, axis=1, keepdims=True)
        probs_low = probs.astype(BF16)
        v2 = two(value)
        attended.append(dot(probs_low[:128], v2[:128]) + dot(probs_low[128:], v2[128:]))
        saved.append((q2, value.astype(BF16), probs, probs_low))
    attended = jnp.concatenate(attended, axis=1).astype(BF16)

    def hand_out(kind, chunk):
        base = S_OUT + 6 * kind
        for i, (x_, z_, to, dst) in enumerate(
            (
                (xx, oh, right, far.at[kind, 0]),
                (xx, zh, left, far.at[kind, 1]),
                (xr, zh, right, near.at[kind, 0]),
                (xl, oh, left, near.at[kind, 1]),
            )
        ):
            stage[kind, i] = chunk(x_, z_).astype(BF16)
            send(stage.at[kind, i], dst, base + i, to)
        for i, (x_, z_) in enumerate(((xr, oh), (xl, zh), (x, oh), (x, zh))):
            hold[kind, i] = chunk(x_, z_)

    def pass_on(kind):
        base = S_OUT + 6 * kind
        for i, to in enumerate((right, left)):
            arrived(far.at[kind, i], base + i)
            stage[kind, 4 + i] = (hold[kind, i] + far[kind, i].astype(F32)).astype(BF16)
            send(stage.at[kind, 4 + i], near.at[kind, 2 + i], base + 4 + i, to)

    def finish(kind):
        base = S_OUT + 6 * kind
        for j, pair in enumerate(((1, 2), (0, 3))):
            total = hold[kind, 2 + j]
            for i in pair:
                arrived(near.at[kind, i], base + 2 + i)
                total = total + near[kind, i].astype(F32)
            hold[kind, 2 + j] = total
            last[kind, j] = total.astype(BF16)
            if j == 0:
                slot = 2 - side if kind else 1 + side
                send(
                    last.at[kind, 0], last_in.at[slot], F_SUM + slot,
                    at(zl_=p + 2 * kind, zh_=oh),
                )
            else:
                send_when(1 - kind, [copy(last.at[kind, 1], last_in.at[0], F_SUM, r1)])

    hand_out(1, lambda x_, j: dot(attended, w[x_, pl.ds(4 * j, 4), :, :, 768:1024].reshape(256, 256), NT))

    for i in range(3):
        cot_arrived(0, i)
    for s, first in ((1, 1), (2, 1), (3, 0)):
        cot_arrived(s, 1 - first)
        cot_arrived(s, 2)
    da = jnp.zeros((128, 256), F32)
    for i, j in blocks:
        da = da + dot(act[2, i, j], w[i, 4 * j : 4 * j + 4, :, :, 768:1024].reshape(256, 256))
    da = da.astype(BF16).astype(F32)

    d_keys, d_values = [], []
    for pair, (q2, value, probs, probs_low) in enumerate(saved):
        da2 = two(da[:, 128 * pair : 128 * pair + 128])
        d_probs = dot(da2, value, NT)
        d_scores = probs * (d_probs - jnp.sum(probs * d_probs, axis=1, keepdims=True))
        d_low = (d_scores * factor).astype(BF16)
        d_keys.append(dot(d_low, q2, TN))
        d_values.append(dot(probs_low, da2, TN))
    d_kv = jnp.concatenate(d_keys + d_values, axis=1).astype(BF16)
    pass_on(1)
    inner = [jnp.zeros((128, 256), F32)]

    def memory_chunk(x_, j):
        v = dot(d_kv, w[x_, pl.ds(4 * j, 4), :, :, 256:768].reshape(256, 512), NT)
        inner[0] = inner[0] + v * (act[0, x_, j].astype(F32) * aux[x_, j, 0:1, :])
        return v

    hand_out(0, memory_chunk)
    own_inner = as_row(jnp.sum(inner[0], axis=1, keepdims=True))
    stat_out[0:1, :] = own_inner
    stat_out[1:8, :] = jnp.zeros((7, 128), F32)
    for i, to in enumerate((right, left, across)):
        send(stat_out, stat_in.at[i], S_STAT + i, to)
    pass_on(0)

    finish(1)
    for i in range(3):
        arrived(stat_in.at[i], S_STAT + i)
    part_inner = own_inner
    for i in range(3):
        part_inner = part_inner + stat_in[i, 0:1, :]
    part_inner = part_inner + jnp.where(zh == 0, c_inner, 0.0)
    last_stat[0:1, :] = part_inner
    last_stat[1:2, :] = as_row(inv_e)
    last_stat[2:8, :] = jnp.zeros((6, 128), F32)
    for i, to in enumerate((r1, r2, r3)):
        send(last_stat, stat_last.at[i], F_STAT + i, to)
    finish(0)

    for i in range(3):
        arrived(stat_last.at[i], F_STAT + i)
        arrived(last_in.at[i], F_SUM + i)
    sums = (
        hold[side, 3] + last_in[1].astype(F32),
        last_in[0].astype(F32) + last_in[2].astype(F32),
    )

    @pl.when(side == 1)
    def _():
        for m, total in ((1, sums[0]), (0, sums[1])):
            out[m] = (rows[m].astype(F32) + total).astype(BF16)

    @pl.when(side == 0)
    def _():
        inners = (
            part_inner + stat_last[1, 0:1, :],
            stat_last[0, 0:1, :] + stat_last[2, 0:1, :],
        )
        invs = (inv_e, as_col(stat_last[0, 1:2, :]))
        for m in range(2):
            weighted = (sums[m] + cot[m].astype(F32)) * gains[0]
            mean = as_col(inners[m]) / D
            inv = invs[m]
            d_rows = inv * weighted - rows[m].astype(F32) * (inv * inv * inv * mean)
            out[m] = d_rows.astype(BF16)

    for one in pending:
        one.wait_send()
    for of_side in (0, 1):

        @pl.when(side == of_side)
        def _(of_side=of_side):
            for one in waits[of_side]:
                one.wait_send()


def hb(v):
    return pltpu.with_memory_space_constraint(v, pltpu.HBM)


def local(segment_rows, row_cotangent, memory_gain, cross_gain, w_query, w_key, w_value, w_out):
    return pl.pallas_call(
        kernel,
        out_shape=jax.ShapeDtypeStruct((2, 128, 256), BF16),
        in_specs=[pl.BlockSpec(memory_space=pl.ANY)] * 8,
        out_specs=pl.BlockSpec(memory_space=pltpu.VMEM),
        scratch_shapes=[
            pltpu.VMEM((2, 128, 256), BF16),
            pltpu.VMEM((2, 128, 256), BF16),
            pltpu.VMEM((2, 1, 256), F32),
            pltpu.VMEM((4, NY, 2, 32, 1024), BF16),
            pltpu.VMEM((3, NX, 2, 128, 256), BF16),
            pltpu.VMEM((NX, 2, 8, 256), F32),
            pltpu.VMEM((2, 4, 128, 256), F32),
            pltpu.VMEM((2, 6, 128, 256), BF16),
            pltpu.VMEM((2, 4, 128, 256), BF16),
            pltpu.VMEM((2, 2, 128, 256), BF16),
            pltpu.VMEM((8, 128), F32),
            pltpu.VMEM((3, 8, 128), F32),
            pltpu.VMEM((2, 2, 128, 256), BF16),
            pltpu.VMEM((3, 128, 256), BF16),
            pltpu.VMEM((8, 128), F32),
            pltpu.VMEM((3, 8, 128), F32),
            pltpu.SemaphoreType.DMA((10,)),
            pltpu.SemaphoreType.DMA((COPIES,)),
            pltpu.SemaphoreType.DMA((COPIES,)),
        ],
        compiler_params=pltpu.CompilerParams(
            collective_id=0, has_side_effects=True, vmem_limit_bytes=48 * 1024 * 1024
        ),
    )(
        hb(segment_rows), hb(row_cotangent), hb(memory_gain.reshape(1, -1)), hb(cross_gain.reshape(1, -1)),
        hb(w_query), hb(w_key), hb(w_value), hb(w_out.T),
    )


def solution(mesh):
    in_specs = (
        P(None, "segment", "head"),
        P(None, "segment", "head"),
        P("head"),
        P("head"),
        P("segment", "head"),
        P("segment", "head"),
        P("segment", "head"),
        P("head", "segment"),
    )
    out_specs = P(None, "segment", "head")
    return jax.shard_map(local, mesh=mesh, in_specs=in_specs, out_specs=out_specs, check_vma=False)
```

```python
import functools

import jax
import jax.numpy as jnp
from jax import lax
from jax.experimental import pallas as pl
from jax.experimental.pallas import tpu as pltpu
from jax.sharding import PartitionSpec as P

D = 2048
HS = 64
EPS = 1e-06
NX = 4
NY = 8
NT = (((1,), (1,)), ((), ()))
TN = (((0,), (0,)), ((), ()))
F32 = jnp.float32
BF16 = jnp.bfloat16

W_Z = 0
W_UP = 3
W_DOWN = 19
W_MATE = 35
W_LAST = 43
A_ROWS = 47
A_COT = 50
A_AUX = 53
X_ROWS = 56
X_COT = 68
X_AUX = 80
S_OUT = 83
S_STAT = 95
F_SUM = 98
F_STAT = 101
COPIES = 104


DIRECT_ROWS = ()
DIRECT_COT = ()


def dot(a, b, dims=(((1,), (0,)), ((), ()))):
    return lax.dot_general(a, b, dims, preferred_element_type=F32)


def kernel(
    rows_h, cot_h, mgain_h, cgain_h, wq, wk, wv, wo, out,
    rows, cot, gains, w, act, aux, hold, stage, near, far, stat_out, stat_in, last, last_in, last_stat,
    stat_last, lsem, ssem, rsem,
):
    seg = lax.axis_index("segment")
    head = lax.axis_index("head")
    c = seg % 2
    y = (seg // 2) % NY
    zl = seg // (2 * NY)
    p = zl % 2
    side = zl // 2
    x = head // 2
    zh = head % 2
    oh = 1 - zh
    other = 1 - side

    def at(x_=x, y_=y, zl_=zl, zh_=zh, c_=c):
        return ((zl_ * NY + y_) * 2 + c_, x_ * 2 + zh_)

    xr, xl, xx = (x + 1) % NX, (x + NX - 1) % NX, (x + 2) % NX
    right, left, across = at(x_=xr), at(x_=xl), at(x_=xx)
    up, down = at(y_=(y + 1) % NY), at(y_=(y + NY - 1) % NY)
    mate = at(c_=1 - c)
    zl_of = (zl, (1 - p) + 2 * side, p + 2 * other, (1 - p) + 2 * other)
    w_to = [None] + [at(zl_=v) for v in zl_of[1:]]
    r1, r2, r3 = at(zl_=zl_of[2]), at(zh_=oh), at(zl_=zl_of[2], zh_=oh)

    def copy(src, dst, number, to):
        return pltpu.make_async_remote_copy(
            src_ref=src, dst_ref=dst, send_sem=ssem.at[number], recv_sem=rsem.at[number],
            device_id=to, device_id_type=pl.DeviceIdType.MESH,
        )

    pending = []

    def send(src, dst, number, to):
        one = copy(src, dst, number, to)
        one.start()
        pending.append(one)

    def arrived(dst, number):
        copy(dst, dst, number, mate).wait_recv()

    eye = lax.broadcasted_iota(jnp.int32, (128, 128), 0) == lax.broadcasted_iota(
        jnp.int32, (128, 128), 1
    )

    def as_row(col):
        return jnp.sum(jnp.where(eye, col, 0.0), axis=0, keepdims=True)

    def as_col(row):
        return jnp.sum(jnp.where(eye, row, 0.0), axis=1, keepdims=True)

    barrier = pltpu.get_barrier_semaphore()
    partners = (right, left, across, up, down, mate, r1, r2, r3, w_to[1], w_to[3])
    for partner in partners:
        pl.semaphore_signal(
            barrier, inc=1, device_id=partner, device_id_type=pl.DeviceIdType.MESH
        )
    own = w.at[zl, y, c]
    places = [(ref, own.at[:, 256 * i : 256 * i + 256]) for i, ref in enumerate((wq, wk, wv, wo))]
    places += [(rows_h, rows), (cot_h, cot)]
    places += [(mgain_h, gains.at[0]), (cgain_h, gains.at[1]), (rows_h.at[side], act.at[side, x, zh])]
    fetch = [
        pltpu.make_async_copy(src, dst, lsem.at[i]) for i, (src, dst) in enumerate(places)
    ]
    fetch_cot = pltpu.make_async_copy(cot_h.at[1], act.at[2, x, zh], lsem.at[len(fetch)])
    for one in fetch:
        one.start()
    encoder, decoder = side == 0, side == 1

    @pl.when(decoder)
    def _():
        fetch_cot.start()

    for one in fetch[:4]:
        one.wait()
    pl.semaphore_wait(barrier, len(partners))

    waits = {0: [], 1: []}

    def send_when(of_side, copies):
        @pl.when(side == of_side)
        def _():
            for one in copies:
                one.start()

        waits[of_side].extend(copies)

    def ring_block(t, d):
        return w.at[zl_of[d], (y + NY + t) % NY, c]

    def forward(t, d):
        if 0 < t < 4 or (t == 4 and d < 2):
            arrived(ring_block(-t, d), W_UP + 4 * (t - 1) + d)
        if t < 3 or (t == 3 and d < 2):
            send(ring_block(-t, d), ring_block(-t, d), W_UP + 4 * t + d, up)
        if 0 < t < 4 or (t == 4 and d >= 2):
            arrived(ring_block(t, d), W_DOWN + 4 * (t - 1) + d)
        if t < 3 or (t == 3 and d >= 2):
            send(ring_block(t, d), ring_block(t, d), W_DOWN + 4 * t + d, down)

    def from_z(d):
        arrived(ring_block(0, d), W_Z + d - 1)
        forward(0, d)

    def share(t):
        block = w.at[:, (y + NY + t) % NY, c]
        send(block, block, W_MATE + t % NY, mate)

    def share_block(t, d):
        block = ring_block(t, d)
        send(block, block, W_LAST + d, mate)

    peers = (right, left, across)
    z_peers = ((r1, other), (r2, side), (r3, other))
    mine, my_cot, my_aux = act.at[side, x, zh], act.at[2, x, zh], aux.at[x, zh]
    kinds = (side, other, side, other)
    z_of = (zh, zh, oh, oh)
    cot_side = (1, 0, 1, 0)
    ring = (xl, xr, xx)

    def rows_block(s, x_):
        return act.at[kinds[s], x_, z_of[s]]

    def cot_block(s, x_):
        return act.at[2, x_, z_of[s]]

    def rows_arrived(s, i):
        arrived(rows_block(s, ring[i]), X_ROWS + 3 * s + i)

    def cot_arrived(s, i):
        @pl.when(side == cot_side[s])
        def _():
            arrived(cot_block(s, ring[i]), X_COT + 3 * s + i)

    def rows_along_z(i):
        to, m = z_peers[i]
        send(rows_h.at[m], mine, A_ROWS + i, to)

    def cot_along_z(i):
        to, m = z_peers[i]
        send_when(1, [copy(cot_h.at[m], my_cot, A_COT + i, to)])

    def rows_along_x(s):
        block = rows_block(s, x)
        arrived(block, A_ROWS + s - 1)
        for i in (0, 1) if s not in DIRECT_ROWS else (2, 0, 1):
            send(block, block, X_ROWS + 3 * s + i, peers[i])

    def cot_along_x(s):
        block = cot_block(s, x)

        @pl.when(side == cot_side[s])
        def _():
            arrived(block, A_COT + s - 1)

        send_when(cot_side[s], [copy(block, block, X_COT + 3 * s + i, peers[i]) for i in ((0, 1) if s not in DIRECT_COT else (2, 0, 1))])

    def rows_relay(s):
        i = 1 if s == 3 else 0
        rows_arrived(s, i)
        block = rows_block(s, ring[i])
        send(block, block, X_ROWS + 3 * s + 2, peers[i])

    def cot_relay(s):
        i = 0 if s == 3 else 1
        cot_arrived(s, i)
        block = cot_block(s, ring[i])
        send_when(cot_side[s], [copy(block, block, X_COT + 3 * s + 2, peers[i])])

    def make_aux():
        for one in fetch[4:]:
            one.wait()

        @pl.when(decoder)
        def _():
            fetch_cot.wait()

        @pl.when(encoder)
        def _():
            aux[x, zh, 0:1, :] = gains[0]
            aux[x, zh, 1:2, :] = gains[1]
            for m in range(2):
                inner = rows[m].astype(F32) * cot[m].astype(F32) * gains[0]
                aux[x, zh, 2:3, 128 * m : 128 * m + 128] = as_row(
                    jnp.sum(inner, axis=1, keepdims=True)
                )
            aux[x, zh, 3:8, :] = jnp.zeros((5, 256), F32)

        send_when(0, [copy(my_aux, my_aux, A_AUX + i, to) for i, to in enumerate((r1, r2, r3))])

    def aux_along_x():
        @pl.when(encoder)
        def _():
            arrived(aux.at[x, oh], A_AUX + 1)

        @pl.when(decoder)
        def _():
            arrived(aux.at[x, zh], A_AUX)
            arrived(aux.at[x, oh], A_AUX + 2)

        for i, to in enumerate(peers):
            send(aux.at[x], aux.at[x], X_AUX + i, to)

    forward(0, 0)
    for d in (1, 2, 3):
        send(own, own, W_Z + d - 1, w_to[d])
    for i, to in enumerate(peers):
        send(rows_h.at[side], mine, X_ROWS + i, to)
    send_when(1, [copy(cot_h.at[1], my_cot, X_COT + i, to) for i, to in enumerate(peers)])
    from_z(1)
    from_z(2)
    from_z(3)
    rows_along_z(0)
    rows_along_z(2)
    rows_along_z(1)
    cot_along_z(1)
    make_aux()
    cot_along_z(0)
    cot_along_z(2)
    share(0)
    forward(1, 0)
    forward(1, 1)
    forward(1, 2)
    forward(1, 3)
    share(1)
    share(-1)
    forward(2, 0)
    forward(2, 1)
    forward(2, 2)
    forward(2, 3)
    share(2)
    share(-2)
    rows_along_x(1)
    rows_along_x(3)
    aux_along_x()
    rows_along_x(2)
    forward(3, 0)
    forward(3, 1)
    forward(3, 2)
    forward(3, 3)
    share(3)
    share(-3)
    rows_relay(1)
    rows_relay(3)
    cot_along_x(1)
    cot_along_x(3)
    cot_along_x(2)
    rows_relay(2)
    forward(4, 0)
    share_block(4, 0)
    forward(4, 1)
    share_block(4, 1)
    forward(4, 2)
    share_block(4, 2)
    forward(4, 3)
    share_block(4, 3)
    cot_relay(1)
    cot_relay(3)
    cot_relay(2)

    for i in range(3):
        rows_arrived(0, i)
        arrived(aux.at[ring[i]], X_AUX + i)
    for s, first in ((1, 0), (2, 0), (3, 1)):
        for i in range(3):
            if s in DIRECT_ROWS or i != first:
                rows_arrived(s, i)
    blocks = [(i // 2, i % 2) for i in range(8)]

    def inverse(kind):
        total = jnp.zeros((128, 256), F32)
        for i, j in blocks:
            v = act[kind, i, j].astype(F32)
            total = total + v * v
        return lax.rsqrt(jnp.sum(total, axis=1, keepdims=True) / D + EPS)

    inv_e = inverse(0)
    inv_x = inverse(1)
    memories = [
        (act[0, i, j].astype(F32) * inv_e * aux[i, j, 0:1, :]).astype(BF16) for i, j in blocks
    ]
    normeds = [
        (act[1, i, j].astype(F32) * inv_x * aux[i, j, 1:2, :]).astype(BF16) for i, j in blocks
    ]
    for t in range(NY):
        if t == 4:
            for d in range(4):
                arrived(w.at[zl_of[d], (y + 4) % NY, 1 - c], W_LAST + d)
        else:
            arrived(w.at[:, (y + t) % NY, 1 - c], W_MATE + t)

    kv = jnp.zeros((128, 512), F32)
    q = jnp.zeros((128, 256), F32)
    c_inner = jnp.zeros((1, 256), F32)
    for (i, j), memory, normed in zip(blocks, memories, normeds):
        part = w.at[i, 4 * j : 4 * j + 4]
        kv = kv + dot(memory, part[:, :, :, 256:768].reshape(256, 512))
        q = q + dot(normed, part[:, :, :, 0:256].reshape(256, 256))
        c_inner = c_inner + aux[i, j, 2:3, :]
    kv = kv.astype(BF16).astype(F32)
    q = q.astype(BF16).astype(F32)
    c_inner = jnp.where(side == 0, c_inner[:, 0:128], c_inner[:, 128:256])

    low = lax.broadcasted_iota(jnp.int32, (128, 128), 1) < HS
    factor = HS ** (-0.5)

    def two(v):
        return jnp.concatenate(
            [jnp.where(low, v, 0.0).astype(BF16), jnp.where(low, 0.0, v).astype(BF16)], axis=0
        )

    attended, saved = [], []
    for pair in range(2):
        lanes = slice(128 * pair, 128 * pair + 128)
        q2 = two(q[:, lanes])
        key = kv[:, lanes].astype(BF16)
        value = kv[:, 256 + 128 * pair : 384 + 128 * pair]
        scores = dot(q2, key, NT) * factor
        e = jnp.exp(scores - jnp.max(scores, axis=1, keepdims=True))
        probs = e / jnp.sum(e, axis=1, keepdims=True)
        probs_low = probs.astype(BF16)
        v2 = two(value)
        attended.append(dot(probs_low[:128], v2[:128]) + dot(probs_low[128:], v2[128:]))
        saved.append((q2, value.astype(BF16), probs, probs_low))
    attended = jnp.concatenate(attended, axis=1).astype(BF16)

    def hand_out(kind, chunk):
        base = S_OUT + 6 * kind
        for i, (x_, z_, to, dst) in enumerate(
            (
                (xx, oh, right, far.at[kind, 0]),
                (xx, zh, left, far.at[kind, 1]),
                (xr, zh, right, near.at[kind, 0]),
                (xl, oh, left, near.at[kind, 1]),
            )
        ):
            stage[kind, i] = chunk(x_, z_).astype(BF16)
            send(stage.at[kind, i], dst, base + i, to)

    def keep(kind, chunk):
        for i, (x_, z_) in enumerate(((xr, oh), (xl, zh), (x, oh), (x, zh))):
            hold[kind, i] = chunk(x_, z_)

    def pass_on(kind):
        base = S_OUT + 6 * kind
        for i, to in enumerate((right, left)):
            arrived(far.at[kind, i], base + i)
            stage[kind, 4 + i] = (hold[kind, i] + far[kind, i].astype(F32)).astype(BF16)
            send(stage.at[kind, 4 + i], near.at[kind, 2 + i], base + 4 + i, to)

    def finish(kind):
        base = S_OUT + 6 * kind
        for j, pair in enumerate(((1, 2), (0, 3))):
            total = hold[kind, 2 + j]
            for i in pair:
                arrived(near.at[kind, i], base + 2 + i)
                total = total + near[kind, i].astype(F32)
            hold[kind, 2 + j] = total
            last[kind, j] = total.astype(BF16)
            if j == 0:
                slot = 2 - side if kind else 1 + side
                send(
                    last.at[kind, 0], last_in.at[slot], F_SUM + slot,
                    at(zl_=p + 2 * kind, zh_=oh),
                )
            else:
                send_when(1 - kind, [copy(last.at[kind, 1], last_in.at[0], F_SUM, r1)])

    def out_chunk(x_, j):
        return dot(attended, w[x_, pl.ds(4 * j, 4), :, :, 768:1024].reshape(256, 256), NT)

    hand_out(1, out_chunk)

    for i in range(3):
        cot_arrived(0, i)
    for s, first in ((1, 1), (2, 1), (3, 0)):
        for i in range(3):
            if s in DIRECT_COT or i != first:
                cot_arrived(s, i)
    da = jnp.zeros((128, 256), F32)
    for i, j in blocks:
        da = da + dot(act[2, i, j], w[i, 4 * j : 4 * j + 4, :, :, 768:1024].reshape(256, 256))
    da = da.astype(BF16).astype(F32)

    d_keys, d_values = [], []
    for pair, (q2, value, probs, probs_low) in enumerate(saved):
        da2 = two(da[:, 128 * pair : 128 * pair + 128])
        d_probs = dot(da2, value, NT)
        d_scores = probs * (d_probs - jnp.sum(probs * d_probs, axis=1, keepdims=True))
        d_low = (d_scores * factor).astype(BF16)
        d_keys.append(dot(d_low, q2, TN))
        d_values.append(dot(probs_low, da2, TN))
    d_kv = jnp.concatenate(d_keys + d_values, axis=1).astype(BF16)
    inner = [jnp.zeros((128, 256), F32)]

    def memory_chunk(x_, j):
        v = dot(d_kv, w[x_, pl.ds(4 * j, 4), :, :, 256:768].reshape(256, 512), NT)
        inner[0] = inner[0] + v * (act[0, x_, j].astype(F32) * aux[x_, j, 0:1, :])
        return v

    hand_out(0, memory_chunk)
    keep(1, out_chunk)
    pass_on(1)
    keep(0, memory_chunk)
    own_inner = as_row(jnp.sum(inner[0], axis=1, keepdims=True))
    stat_out[0:1, :] = own_inner
    stat_out[1:8, :] = jnp.zeros((7, 128), F32)
    for i, to in enumerate((right, left, across)):
        send(stat_out, stat_in.at[i], S_STAT + i, to)
    pass_on(0)

    finish(1)
    for i in range(3):
        arrived(stat_in.at[i], S_STAT + i)
    part_inner = own_inner
    for i in range(3):
        part_inner = part_inner + stat_in[i, 0:1, :]
    part_inner = part_inner + jnp.where(zh == 0, c_inner, 0.0)
    last_stat[0:1, :] = part_inner
    last_stat[1:2, :] = as_row(inv_e)
    last_stat[2:8, :] = jnp.zeros((6, 128), F32)
    for i, to in enumerate((r1, r2, r3)):
        send(last_stat, stat_last.at[i], F_STAT + i, to)
    finish(0)

    for i in range(3):
        arrived(stat_last.at[i], F_STAT + i)
        arrived(last_in.at[i], F_SUM + i)
    sums = (
        hold[side, 3] + last_in[1].astype(F32),
        last_in[0].astype(F32) + last_in[2].astype(F32),
    )

    @pl.when(side == 1)
    def _():
        for m, total in ((1, sums[0]), (0, sums[1])):
            out[m] = (rows[m].astype(F32) + total).astype(BF16)

    @pl.when(side == 0)
    def _():
        inners = (
            part_inner + stat_last[1, 0:1, :],
            stat_last[0, 0:1, :] + stat_last[2, 0:1, :],
        )
        invs = (inv_e, as_col(stat_last[0, 1:2, :]))
        for m in range(2):
            weighted = (sums[m] + cot[m].astype(F32)) * gains[0]
            mean = as_col(inners[m]) / D
            inv = invs[m]
            d_rows = inv * weighted - rows[m].astype(F32) * (inv * inv * inv * mean)
            out[m] = d_rows.astype(BF16)

    for one in pending:
        one.wait_send()
    for of_side in (0, 1):

        @pl.when(side == of_side)
        def _(of_side=of_side):
            for one in waits[of_side]:
                one.wait_send()


def hb(v):
    return pltpu.with_memory_space_constraint(v, pltpu.HBM)


def local(segment_rows, row_cotangent, memory_gain, cross_gain, w_query, w_key, w_value, w_out):
    return pl.pallas_call(
        kernel,
        out_shape=jax.ShapeDtypeStruct((2, 128, 256), BF16),
        in_specs=[pl.BlockSpec(memory_space=pl.ANY)] * 8,
        out_specs=pl.BlockSpec(memory_space=pltpu.VMEM),
        scratch_shapes=[
            pltpu.VMEM((2, 128, 256), BF16),
            pltpu.VMEM((2, 128, 256), BF16),
            pltpu.VMEM((2, 1, 256), F32),
            pltpu.VMEM((4, NY, 2, 32, 1024), BF16),
            pltpu.VMEM((3, NX, 2, 128, 256), BF16),
            pltpu.VMEM((NX, 2, 8, 256), F32),
            pltpu.VMEM((2, 4, 128, 256), F32),
            pltpu.VMEM((2, 6, 128, 256), BF16),
            pltpu.VMEM((2, 4, 128, 256), BF16),
            pltpu.VMEM((2, 2, 128, 256), BF16),
            pltpu.VMEM((8, 128), F32),
            pltpu.VMEM((3, 8, 128), F32),
            pltpu.VMEM((2, 2, 128, 256), BF16),
            pltpu.VMEM((3, 128, 256), BF16),
            pltpu.VMEM((8, 128), F32),
            pltpu.VMEM((3, 8, 128), F32),
            pltpu.SemaphoreType.DMA((10,)),
            pltpu.SemaphoreType.DMA((COPIES,)),
            pltpu.SemaphoreType.DMA((COPIES,)),
        ],
        compiler_params=pltpu.CompilerParams(
            collective_id=0, has_side_effects=True, vmem_limit_bytes=48 * 1024 * 1024
        ),
    )(
        hb(segment_rows), hb(row_cotangent), hb(memory_gain.reshape(1, -1)), hb(cross_gain.reshape(1, -1)),
        hb(w_query), hb(w_key), hb(w_value), hb(w_out.T),
    )


def solution(mesh):
    in_specs = (
        P(None, "segment", "head"),
        P(None, "segment", "head"),
        P("head"),
        P("head"),
        P("segment", "head"),
        P("segment", "head"),
        P("segment", "head"),
        P("head", "segment"),
    )
    out_specs = P(None, "segment", "head")
    return jax.shard_map(local, mesh=mesh, in_specs=in_specs, out_specs=out_specs, check_vma=False)
```

```python
import functools

import jax
import jax.numpy as jnp
from jax import lax
from jax.experimental import pallas as pl
from jax.experimental.pallas import tpu as pltpu
from jax.sharding import PartitionSpec as P

D = 2048
HS = 64
EPS = 1e-06
NX = 4
NY = 8
NT = (((1,), (1,)), ((), ()))
TN = (((0,), (0,)), ((), ()))
F32 = jnp.float32
BF16 = jnp.bfloat16

W_Z = 0
W_UP = 3
W_DOWN = 19
W_MATE = 35
W_LAST = 43
A_ROWS = 47
A_COT = 50
A_AUX = 53
X_ROWS = 56
X_COT = 68
X_AUX = 80
S_OUT = 83
S_STAT = 95
F_SUM = 98
F_STAT = 101
COPIES = 104


DIRECT_ROWS = ()
DIRECT_COT = ()


def dot(a, b, dims=(((1,), (0,)), ((), ()))):
    return lax.dot_general(a, b, dims, preferred_element_type=F32)


def kernel(
    rows_h, cot_h, mgain_h, cgain_h, wq, wk, wv, wo, out,
    rows, cot, gains, w, act, aux, hold, stage, near, far, stat_out, stat_in, last, last_in, last_stat,
    stat_last, lsem, ssem, rsem, answer,
):
    seg = lax.axis_index("segment")
    head = lax.axis_index("head")
    c = seg % 2
    y = (seg // 2) % NY
    zl = seg // (2 * NY)
    p = zl % 2
    side = zl // 2
    x = head // 2
    zh = head % 2
    oh = 1 - zh
    other = 1 - side

    def at(x_=x, y_=y, zl_=zl, zh_=zh, c_=c):
        return ((zl_ * NY + y_) * 2 + c_, x_ * 2 + zh_)

    xr, xl, xx = (x + 1) % NX, (x + NX - 1) % NX, (x + 2) % NX
    right, left, across = at(x_=xr), at(x_=xl), at(x_=xx)
    up, down = at(y_=(y + 1) % NY), at(y_=(y + NY - 1) % NY)
    mate = at(c_=1 - c)
    zl_of = (zl, (1 - p) + 2 * side, p + 2 * other, (1 - p) + 2 * other)
    w_to = [None] + [at(zl_=v) for v in zl_of[1:]]
    r1, r2, r3 = at(zl_=zl_of[2]), at(zh_=oh), at(zl_=zl_of[2], zh_=oh)

    def copy(src, dst, number, to):
        return pltpu.make_async_remote_copy(
            src_ref=src, dst_ref=dst, send_sem=ssem.at[number], recv_sem=rsem.at[number],
            device_id=to, device_id_type=pl.DeviceIdType.MESH,
        )

    pending = []

    def send(src, dst, number, to):
        one = copy(src, dst, number, to)
        one.start()
        pending.append(one)

    def arrived(dst, number):
        copy(dst, dst, number, mate).wait_recv()

    eye = lax.broadcasted_iota(jnp.int32, (128, 128), 0) == lax.broadcasted_iota(
        jnp.int32, (128, 128), 1
    )

    def as_row(col):
        return jnp.sum(jnp.where(eye, col, 0.0), axis=0, keepdims=True)

    def as_col(row):
        return jnp.sum(jnp.where(eye, row, 0.0), axis=1, keepdims=True)

    barrier = pltpu.get_barrier_semaphore()
    partners = (right, left, across, up, down, mate, r1, w_to[1], w_to[3])

    def greet(semaphore, devices):
        for device in devices:
            pl.semaphore_signal(
                semaphore, inc=1, device_id=device, device_id_type=pl.DeviceIdType.MESH
            )

    greet(barrier, partners)

    @pl.when(zh == 0)
    def _():
        greet(barrier, (r2, r3))

    own = w.at[zl, y, c]
    places = [(ref, own.at[:, 256 * i : 256 * i + 256]) for i, ref in enumerate((wq, wk, wv, wo))]
    places += [(rows_h, rows), (cot_h, cot)]
    places += [(mgain_h, gains.at[0]), (cgain_h, gains.at[1]), (rows_h.at[side], act.at[side, x, zh])]
    fetch = [
        pltpu.make_async_copy(src, dst, lsem.at[i]) for i, (src, dst) in enumerate(places)
    ]
    fetch_cot = pltpu.make_async_copy(cot_h.at[1], act.at[2, x, zh], lsem.at[len(fetch)])
    for one in fetch:
        one.start()
    encoder, decoder = side == 0, side == 1

    @pl.when(decoder)
    def _():
        fetch_cot.start()

    for one in fetch[:4]:
        one.wait()
    pl.semaphore_wait(barrier, len(partners) + 2 * zh)

    @pl.when(zh == 1)
    def _():
        greet(answer, (r2, r3))


    waits = {0: [], 1: []}

    def send_when(of_side, copies):
        @pl.when(side == of_side)
        def _():
            for one in copies:
                one.start()

        waits[of_side].extend(copies)

    def ring_block(t, d):
        return w.at[zl_of[d], (y + NY + t) % NY, c]

    def forward(t, d):
        if 0 < t < 4 or (t == 4 and d < 2):
            arrived(ring_block(-t, d), W_UP + 4 * (t - 1) + d)
        if t < 3 or (t == 3 and d < 2):
            send(ring_block(-t, d), ring_block(-t, d), W_UP + 4 * t + d, up)
        if 0 < t < 4 or (t == 4 and d >= 2):
            arrived(ring_block(t, d), W_DOWN + 4 * (t - 1) + d)
        if t < 3 or (t == 3 and d >= 2):
            send(ring_block(t, d), ring_block(t, d), W_DOWN + 4 * t + d, down)

    def from_z(d):
        arrived(ring_block(0, d), W_Z + d - 1)
        forward(0, d)

    def share(t):
        block = w.at[:, (y + NY + t) % NY, c]
        send(block, block, W_MATE + t % NY, mate)

    def share_block(t, d):
        block = ring_block(t, d)
        send(block, block, W_LAST + d, mate)

    peers = (right, left, across)
    z_peers = ((r1, other), (r2, side), (r3, other))
    mine, my_cot, my_aux = act.at[side, x, zh], act.at[2, x, zh], aux.at[x, zh]
    kinds = (side, other, side, other)
    z_of = (zh, zh, oh, oh)
    cot_side = (1, 0, 1, 0)
    ring = (xl, xr, xx)

    def rows_block(s, x_):
        return act.at[kinds[s], x_, z_of[s]]

    def cot_block(s, x_):
        return act.at[2, x_, z_of[s]]

    def rows_arrived(s, i):
        arrived(rows_block(s, ring[i]), X_ROWS + 3 * s + i)

    def cot_arrived(s, i):
        @pl.when(side == cot_side[s])
        def _():
            arrived(cot_block(s, ring[i]), X_COT + 3 * s + i)

    def rows_along_z(i):
        to, m = z_peers[i]
        send(rows_h.at[m], mine, A_ROWS + i, to)

    def cot_along_z(i):
        to, m = z_peers[i]
        send_when(1, [copy(cot_h.at[m], my_cot, A_COT + i, to)])

    def rows_along_x(s):
        block = rows_block(s, x)
        arrived(block, A_ROWS + s - 1)
        for i in (0, 1) if s not in DIRECT_ROWS else (2, 0, 1):
            send(block, block, X_ROWS + 3 * s + i, peers[i])

    def cot_along_x(s):
        block = cot_block(s, x)

        @pl.when(side == cot_side[s])
        def _():
            arrived(block, A_COT + s - 1)

        send_when(cot_side[s], [copy(block, block, X_COT + 3 * s + i, peers[i]) for i in ((0, 1) if s not in DIRECT_COT else (2, 0, 1))])

    def rows_relay(s):
        i = 1 if s == 3 else 0
        rows_arrived(s, i)
        block = rows_block(s, ring[i])
        send(block, block, X_ROWS + 3 * s + 2, peers[i])

    def cot_relay(s):
        i = 0 if s == 3 else 1
        cot_arrived(s, i)
        block = cot_block(s, ring[i])
        send_when(cot_side[s], [copy(block, block, X_COT + 3 * s + 2, peers[i])])

    def make_aux():
        for one in fetch[4:]:
            one.wait()

        @pl.when(decoder)
        def _():
            fetch_cot.wait()

        @pl.when(encoder)
        def _():
            aux[x, zh, 0:1, :] = gains[0]
            aux[x, zh, 1:2, :] = gains[1]
            for m in range(2):
                inner = rows[m].astype(F32) * cot[m].astype(F32) * gains[0]
                aux[x, zh, 2:3, 128 * m : 128 * m + 128] = as_row(
                    jnp.sum(inner, axis=1, keepdims=True)
                )
            aux[x, zh, 3:8, :] = jnp.zeros((5, 256), F32)

        send_when(0, [copy(my_aux, my_aux, A_AUX + i, to) for i, to in enumerate((r1, r2, r3))])

    def aux_along_x():
        @pl.when(encoder)
        def _():
            arrived(aux.at[x, oh], A_AUX + 1)

        @pl.when(decoder)
        def _():
            arrived(aux.at[x, zh], A_AUX)
            arrived(aux.at[x, oh], A_AUX + 2)

        for i, to in enumerate(peers):
            send(aux.at[x], aux.at[x], X_AUX + i, to)

    forward(0, 0)
    for d in (1, 2, 3):
        send(own, own, W_Z + d - 1, w_to[d])
    for i, to in enumerate(peers):
        send(rows_h.at[side], mine, X_ROWS + i, to)
    send_when(1, [copy(cot_h.at[1], my_cot, X_COT + i, to) for i, to in enumerate(peers)])
    from_z(1)
    from_z(2)
    from_z(3)

    @pl.when(zh == 0)
    def _():
        pl.semaphore_wait(answer, 2)

    rows_along_z(0)
    rows_along_z(2)
    rows_along_z(1)
    cot_along_z(1)
    make_aux()
    cot_along_z(0)
    cot_along_z(2)
    share(0)
    forward(1, 0)
    forward(1, 1)
    forward(1, 2)
    forward(1, 3)
    share(1)
    share(-1)
    forward(2, 0)
    forward(2, 1)
    rows_along_x(1)
    forward(2, 2)
    rows_along_x(3)
    forward(2, 3)
    share(2)
    share(-2)
    aux_along_x()
    rows_along_x(2)
    forward(3, 0)
    forward(3, 1)
    forward(3, 2)
    forward(3, 3)
    share(3)
    share(-3)
    rows_relay(1)
    rows_relay(3)
    cot_along_x(1)
    cot_along_x(3)
    cot_along_x(2)
    rows_relay(2)
    forward(4, 0)
    share_block(4, 0)
    forward(4, 1)
    share_block(4, 1)
    forward(4, 2)
    share_block(4, 2)
    forward(4, 3)
    share_block(4, 3)
    cot_relay(1)
    cot_relay(3)
    cot_relay(2)

    for i in range(3):
        rows_arrived(0, i)
        arrived(aux.at[ring[i]], X_AUX + i)
    for s, first in ((1, 0), (2, 0), (3, 1)):
        for i in range(3):
            if s in DIRECT_ROWS or i != first:
                rows_arrived(s, i)
    blocks = [(i // 2, i % 2) for i in range(8)]

    def inverse(kind):
        total = jnp.zeros((128, 256), F32)
        for i, j in blocks:
            v = act[kind, i, j].astype(F32)
            total = total + v * v
        return lax.rsqrt(jnp.sum(total, axis=1, keepdims=True) / D + EPS)

    inv_e = inverse(0)
    inv_x = inverse(1)
    memories = [
        (act[0, i, j].astype(F32) * inv_e * aux[i, j, 0:1, :]).astype(BF16) for i, j in blocks
    ]
    normeds = [
        (act[1, i, j].astype(F32) * inv_x * aux[i, j, 1:2, :]).astype(BF16) for i, j in blocks
    ]
    for t in range(NY):
        if t == 4:
            for d in range(4):
                arrived(w.at[zl_of[d], (y + 4) % NY, 1 - c], W_LAST + d)
        else:
            arrived(w.at[:, (y + t) % NY, 1 - c], W_MATE + t)

    kv = jnp.zeros((128, 512), F32)
    q = jnp.zeros((128, 256), F32)
    c_inner = jnp.zeros((1, 256), F32)
    for (i, j), memory, normed in zip(blocks, memories, normeds):
        part = w.at[i, 4 * j : 4 * j + 4]
        kv = kv + dot(memory, part[:, :, :, 256:768].reshape(256, 512))
        q = q + dot(normed, part[:, :, :, 0:256].reshape(256, 256))
        c_inner = c_inner + aux[i, j, 2:3, :]
    kv = kv.astype(BF16).astype(F32)
    q = q.astype(BF16).astype(F32)
    c_inner = jnp.where(side == 0, c_inner[:, 0:128], c_inner[:, 128:256])

    low = lax.broadcasted_iota(jnp.int32, (128, 128), 1) < HS
    factor = HS ** (-0.5)

    def two(v):
        return jnp.concatenate(
            [jnp.where(low, v, 0.0).astype(BF16), jnp.where(low, 0.0, v).astype(BF16)], axis=0
        )

    attended, saved = [], []
    for pair in range(2):
        lanes = slice(128 * pair, 128 * pair + 128)
        q2 = two(q[:, lanes])
        key = kv[:, lanes].astype(BF16)
        value = kv[:, 256 + 128 * pair : 384 + 128 * pair]
        scores = dot(q2, key, NT) * factor
        e = jnp.exp(scores - jnp.max(scores, axis=1, keepdims=True))
        probs = e / jnp.sum(e, axis=1, keepdims=True)
        probs_low = probs.astype(BF16)
        v2 = two(value)
        attended.append(dot(probs_low[:128], v2[:128]) + dot(probs_low[128:], v2[128:]))
        saved.append((q2, value.astype(BF16), probs, probs_low))
    attended = jnp.concatenate(attended, axis=1).astype(BF16)

    def hand_out(kind, chunk):
        base = S_OUT + 6 * kind
        for i, (x_, z_, to, dst) in enumerate(
            (
                (xx, oh, right, far.at[kind, 0]),
                (xx, zh, left, far.at[kind, 1]),
                (xr, zh, right, near.at[kind, 0]),
                (xl, oh, left, near.at[kind, 1]),
            )
        ):
            stage[kind, i] = chunk(x_, z_).astype(BF16)
            send(stage.at[kind, i], dst, base + i, to)

    def keep(kind, chunk):
        for i, (x_, z_) in enumerate(((xr, oh), (xl, zh), (x, oh), (x, zh))):
            hold[kind, i] = chunk(x_, z_)

    def pass_on(kind):
        base = S_OUT + 6 * kind
        for i, to in enumerate((right, left)):
            arrived(far.at[kind, i], base + i)
            stage[kind, 4 + i] = (hold[kind, i] + far[kind, i].astype(F32)).astype(BF16)
            send(stage.at[kind, 4 + i], near.at[kind, 2 + i], base + 4 + i, to)

    def finish(kind):
        base = S_OUT + 6 * kind
        for j, pair in enumerate(((1, 2), (0, 3))):
            total = hold[kind, 2 + j]
            for i in pair:
                arrived(near.at[kind, i], base + 2 + i)
                total = total + near[kind, i].astype(F32)
            hold[kind, 2 + j] = total
            last[kind, j] = total.astype(BF16)
            if j == 0:
                slot = 2 - side if kind else 1 + side
                send(
                    last.at[kind, 0], last_in.at[slot], F_SUM + slot,
                    at(zl_=p + 2 * kind, zh_=oh),
                )
            else:
                send_when(1 - kind, [copy(last.at[kind, 1], last_in.at[0], F_SUM, r1)])

    def out_chunk(x_, j):
        return dot(attended, w[x_, pl.ds(4 * j, 4), :, :, 768:1024].reshape(256, 256), NT)

    hand_out(1, out_chunk)

    for i in range(3):
        cot_arrived(0, i)
    for s, first in ((1, 1), (2, 1), (3, 0)):
        for i in range(3):
            if s in DIRECT_COT or i != first:
                cot_arrived(s, i)
    da = jnp.zeros((128, 256), F32)
    for i, j in blocks:
        da = da + dot(act[2, i, j], w[i, 4 * j : 4 * j + 4, :, :, 768:1024].reshape(256, 256))
    da = da.astype(BF16).astype(F32)

    d_keys, d_values = [], []
    for pair, (q2, value, probs, probs_low) in enumerate(saved):
        da2 = two(da[:, 128 * pair : 128 * pair + 128])
        d_probs = dot(da2, value, NT)
        d_scores = probs * (d_probs - jnp.sum(probs * d_probs, axis=1, keepdims=True))
        d_low = (d_scores * factor).astype(BF16)
        d_keys.append(dot(d_low, q2, TN))
        d_values.append(dot(probs_low, da2, TN))
    d_kv = jnp.concatenate(d_keys + d_values, axis=1).astype(BF16)
    inner = [jnp.zeros((128, 256), F32)]

    def memory_chunk(x_, j):
        v = dot(d_kv, w[x_, pl.ds(4 * j, 4), :, :, 256:768].reshape(256, 512), NT)
        inner[0] = inner[0] + v * (act[0, x_, j].astype(F32) * aux[x_, j, 0:1, :])
        return v

    hand_out(0, memory_chunk)
    keep(1, out_chunk)
    pass_on(1)
    keep(0, memory_chunk)
    own_inner = as_row(jnp.sum(inner[0], axis=1, keepdims=True))
    stat_out[0:1, :] = own_inner
    stat_out[1:8, :] = jnp.zeros((7, 128), F32)
    for i, to in enumerate((right, left, across)):
        send(stat_out, stat_in.at[i], S_STAT + i, to)
    pass_on(0)

    finish(1)
    for i in range(3):
        arrived(stat_in.at[i], S_STAT + i)
    part_inner = own_inner
    for i in range(3):
        part_inner = part_inner + stat_in[i, 0:1, :]
    part_inner = part_inner + jnp.where(zh == 0, c_inner, 0.0)
    last_stat[0:1, :] = part_inner
    last_stat[1:2, :] = as_row(inv_e)
    last_stat[2:8, :] = jnp.zeros((6, 128), F32)
    for i, to in enumerate((r1, r2, r3)):
        send(last_stat, stat_last.at[i], F_STAT + i, to)
    finish(0)

    for i in range(3):
        arrived(stat_last.at[i], F_STAT + i)
        arrived(last_in.at[i], F_SUM + i)
    sums = (
        hold[side, 3] + last_in[1].astype(F32),
        last_in[0].astype(F32) + last_in[2].astype(F32),
    )

    @pl.when(side == 1)
    def _():
        for m, total in ((1, sums[0]), (0, sums[1])):
            out[m] = (rows[m].astype(F32) + total).astype(BF16)

    @pl.when(side == 0)
    def _():
        inners = (
            part_inner + stat_last[1, 0:1, :],
            stat_last[0, 0:1, :] + stat_last[2, 0:1, :],
        )
        invs = (inv_e, as_col(stat_last[0, 1:2, :]))
        for m in range(2):
            weighted = (sums[m] + cot[m].astype(F32)) * gains[0]
            mean = as_col(inners[m]) / D
            inv = invs[m]
            d_rows = inv * weighted - rows[m].astype(F32) * (inv * inv * inv * mean)
            out[m] = d_rows.astype(BF16)

    for one in pending:
        one.wait_send()
    for of_side in (0, 1):

        @pl.when(side == of_side)
        def _(of_side=of_side):
            for one in waits[of_side]:
                one.wait_send()


def hb(v):
    return pltpu.with_memory_space_constraint(v, pltpu.HBM)


def local(segment_rows, row_cotangent, memory_gain, cross_gain, w_query, w_key, w_value, w_out):
    return pl.pallas_call(
        kernel,
        out_shape=jax.ShapeDtypeStruct((2, 128, 256), BF16),
        in_specs=[pl.BlockSpec(memory_space=pl.ANY)] * 8,
        out_specs=pl.BlockSpec(memory_space=pltpu.VMEM),
        scratch_shapes=[
            pltpu.VMEM((2, 128, 256), BF16),
            pltpu.VMEM((2, 128, 256), BF16),
            pltpu.VMEM((2, 1, 256), F32),
            pltpu.VMEM((4, NY, 2, 32, 1024), BF16),
            pltpu.VMEM((3, NX, 2, 128, 256), BF16),
            pltpu.VMEM((NX, 2, 8, 256), F32),
            pltpu.VMEM((2, 4, 128, 256), F32),
            pltpu.VMEM((2, 6, 128, 256), BF16),
            pltpu.VMEM((2, 4, 128, 256), BF16),
            pltpu.VMEM((2, 2, 128, 256), BF16),
            pltpu.VMEM((8, 128), F32),
            pltpu.VMEM((3, 8, 128), F32),
            pltpu.VMEM((2, 2, 128, 256), BF16),
            pltpu.VMEM((3, 128, 256), BF16),
            pltpu.VMEM((8, 128), F32),
            pltpu.VMEM((3, 8, 128), F32),
            pltpu.SemaphoreType.DMA((10,)),
            pltpu.SemaphoreType.DMA((COPIES,)),
            pltpu.SemaphoreType.DMA((COPIES,)),
            pltpu.SemaphoreType.REGULAR,
        ],
        compiler_params=pltpu.CompilerParams(
            collective_id=0, has_side_effects=True, vmem_limit_bytes=48 * 1024 * 1024
        ),
    )(
        hb(segment_rows), hb(row_cotangent), hb(memory_gain.reshape(1, -1)), hb(cross_gain.reshape(1, -1)),
        hb(w_query), hb(w_key), hb(w_value), hb(w_out.T),
    )


def solution(mesh):
    in_specs = (
        P(None, "segment", "head"),
        P(None, "segment", "head"),
        P("head"),
        P("head"),
        P("segment", "head"),
        P("segment", "head"),
        P("segment", "head"),
        P("head", "segment"),
    )
    out_specs = P(None, "segment", "head")
    return jax.shard_map(local, mesh=mesh, in_specs=in_specs, out_specs=out_specs, check_vma=False)
```
